256 devices in a mesh: head: 4 (over y), expert: 32 (over z, x), batch: 2 (over core).
Axes of the slice: x: 4, y: 4, z: 8, core: 2. Of those that a mesh axis runs over, the one named last changes fastest.
Arguments:
- tokens: bfloat16 [512, 4096], P('batch', 'expert'), may hold values from -3 to 3
- attn_gain: bfloat16 [4096], P('expert'), may hold values from 0.099609375 to 1.8984375
- w_query: bfloat16 [4096, 8192], P('expert', 'head'), may hold values from -0.09375 to 0.09375
- q_gain: bfloat16 [128], replicated, may hold values from 0.099609375 to 1.8984375
- cached_keys: bfloat16 [131072, 512], P('expert', 'head'), may hold values from -400 to 400
- prefix_values: bfloat16 [131072, 512], P('expert', 'head'), may hold values from -6 to 6
- output_weight: bfloat16 [8192, 4096], P('head', 'expert'), may hold values from -0.125 to 0.125
- post_gain: bfloat16 [4096], replicated, may hold values from 0.099609375 to 1.8984375
- routes: int32 [512, 8], P('batch'), may hold values from 0 to 63, all different within a row; in each aligned block of 8 rows (0 to 7, 8 to 15, ...) at most 2 rows name the same one
- route_gates: float32 [512, 8], P('batch'), may hold values from 0.1 to 1
- w_gate: bfloat16 [64, 4096, 1536], P(('expert', 'batch'), None, 'head'), may hold values from -0.09375 to 0.09375
- w_up: bfloat16 [64, 4096, 1536], P(('expert', 'batch'), None, 'head'), may hold values from -0.09375 to 0.09375
- w_down: bfloat16 [64, 1536, 4096], P(('expert', 'batch'), 'head'), may hold values from -0.21875 to 0.21875
Outputs:
- layer_out: bfloat16 [512, 4096], P('batch', 'expert')
The draws below stay inside these ranges and needn't reach their ends.
Inputs may be any that keep to these rules, and one draw needn't show every extreme that they name: `routes`: each row names 8 different experts; in each aligned block of 8 rows no expert is named by more than 2 rows.
All inputs are finite; a program needn't handle non-finite values.
Results may differ from the reference program's by a relative error of at most 0.019.
The reference program's roundings to bfloat16 on the way count: a program that leaves them out, or rounds other values in their place, can miss the bound.
Values may be sent and summed in bfloat16 or wider, within the bound.
A program may use at most 192 MiB of HBM per device.

```python
import math
import jax
import jax.numpy as jnp
import numpy as np
from jax import lax

MODEL_DIM = 4096
QUERY_HEADS = 64
KEY_VALUE_HEADS = 4
HEAD_DIM = 128
FF = 1536
TOP = 8
TOK_DEV = 8
TOKEN_TOTAL = 512
PREFIX_LENGTH = 131072
EXPERTS = 64
CAP = 2


def draw_cached_keys(key, part):
    key = jax.random.fold_in(key, 7)
    base_key, pick_key, loud_key, group_key, side_key = jax.random.split(key, 5)
    complete_shape = (PREFIX_LENGTH, KEY_VALUE_HEADS * HEAD_DIM)
    chosen = jax.random.randint(pick_key, (2,), 0, PREFIX_LENGTH)
    places = jnp.arange(PREFIX_LENGTH, dtype=jnp.int32)[:, None]
    loud_rows = jnp.any(places == chosen[None, :], axis=1, keepdims=True)
    twin_rows = jnp.roll(loud_rows, 1, axis=0)
    loud_group = jax.random.randint(group_key, (), 0, KEY_VALUE_HEADS)
    columns = jnp.arange(KEY_VALUE_HEADS * HEAD_DIM, dtype=jnp.int32)[None, :] // HEAD_DIM
    in_group = columns == loud_group
    side_keys = jnp.clip(jax.random.normal(side_key, complete_shape, jnp.float32) * 9.0, -54.0, 54.0)
    entries = jnp.clip(jax.random.normal(base_key, complete_shape, jnp.float32) * 3.0, -18.0, 18.0)
    strong_keys = jnp.clip(jax.random.normal(loud_key, complete_shape, jnp.float32) * 80.0, -320.0, 320.0)
    loud_keys = jnp.where(in_group, strong_keys, side_keys)
    twin_keys = jnp.roll(loud_keys, 1, axis=0) * 1.01
    drawn = jnp.where(loud_rows, loud_keys, jnp.where(twin_rows, twin_keys, entries))
    return drawn.astype(jnp.bfloat16)


def steps_of(key, dims, cuts, low, top_value):
    loudness = 1.0
    for position, parts in cuts:
        heights = jax.random.uniform(jax.random.fold_in(jax.random.fold_in(key, 6), position), (parts,), jnp.float32, low / len(cuts), top_value / len(cuts))
        loudness = loudness * jnp.repeat(jnp.exp(heights), dims[position] // parts).reshape((-1,) + (1,) * (len(dims) - 1 - position))
    return loudness


def routed_block(rng, own, number, rows, count, top, bound, skew):
    order = jax.random.permutation(rng, count)
    heavy_load, common = shares(count, rows * top, bound, skew, True), shares(count, rows * top, bound, skew, False)
    places = jnp.arange(count)

    def named(lengths, turn):
        used = int((lengths > 0).sum())
        fixed = max(1, used // 4)
        shifted = fixed + (places - fixed + turn * (used - fixed)) % max(1, count - fixed)
        return jnp.zeros((count,), jnp.int32).at[order[jnp.where(places < fixed, places, shifted)]].set(jnp.asarray(lengths, jnp.int32))

    lengths = jnp.where(number % 4 == 0, named(heavy_load, number // 4), named(common, number - number // 4 - 1))
    mixed = jax.random.permutation(jax.random.fold_in(own, 3), count)
    donor, taker = mixed[0:count // 2 * 2:2], mixed[1:count // 2 * 2:2]
    margin = jnp.minimum(lengths[donor] - 1, bound - lengths[taker]) // 2
    margin = jnp.where((donor == order[0]) | (taker == order[0]) | (lengths[taker] == 0), 0, jnp.maximum(margin, 0))
    shifted = jax.random.randint(jax.random.fold_in(own, 4), (count // 2,), 0, 1 << 20) % (margin + 1)
    lengths = lengths.at[donor].add(-shifted).at[taker].add(shifted)
    labels = jnp.searchsorted(jnp.cumsum(lengths), jnp.arange(rows * top), side="right").astype(jnp.int32)
    listing = labels.reshape(top, rows).T
    listing = listing[jax.random.permutation(jax.random.fold_in(own, 1), rows)]
    turn = jax.random.randint(jax.random.fold_in(own, 2), (rows, 1), 0, top)
    return jnp.take_along_axis(listing, (jnp.arange(top)[None, :] + turn) % top, axis=1)


def shares(number_of, total, most, slope, full):
    weights = [(1 << 20) // math.isqrt(rank ** slope) + 1 for rank in range(1, number_of + 1)]
    largest = most if full else min(most, max(-(-total // number_of), total * weights[0] // sum(weights)))
    least = 1 if total - largest >= number_of - 1 else 0
    holding, surplus = [largest] + [least] * (number_of - 1), total - largest - least * (number_of - 1)
    while surplus > 0:
        free = [i for i in range(1, number_of) if holding[i] < largest] or [i for i in range(1, number_of) if holding[i] < most]
        whole, budget = sum([weights[i] for i in free]), surplus
        for i in free:
            more = min(most - holding[i], max(1, budget * weights[i] // whole), surplus)
            holding[i] = holding[i] + more
            surplus = surplus - more
    return np.array(holding)


def normal_values(rng, shape, deviation, limit, cuts=(), kind=jnp.bfloat16):
    values = jax.random.normal(rng, shape, jnp.float32) * deviation
    if len(cuts) > 0:
        values = steps_of(rng, shape, cuts, -0.22, 0.18) * values
    return jnp.clip(values, min=-limit, max=limit).astype(kind)


def setup_inputs(seed: int = 0) -> dict:
    seeds = jax.random.split(jax.random.key(seed), 14)
    tokens = normal_values(seeds[0], (TOKEN_TOTAL, MODEL_DIM), 0.2, 3.0, ((0, 2), (1, 32)))
    attn_gain = jnp.clip(1.0 + 0.18 * jax.random.normal(seeds[1], (MODEL_DIM,), jnp.float32), 0.099609375, 1.8984375).astype(jnp.bfloat16)
    w_query = normal_values(seeds[2], (MODEL_DIM, QUERY_HEADS * HEAD_DIM), MODEL_DIM ** -0.5, 0.09375, ((0, 32), (1, 4)))
    q_gain = jnp.clip(1.0 + 0.18 * jax.random.normal(seeds[3], (HEAD_DIM,), jnp.float32), 0.099609375, 1.8984375).astype(jnp.bfloat16)
    cached_keys = draw_cached_keys(jax.random.fold_in(seeds[13], 71), 0)
    prefix_values = normal_values(seeds[5], (PREFIX_LENGTH, KEY_VALUE_HEADS * HEAD_DIM), 1.0, 6.0, ((0, 32), (1, 4)))
    output_weight = normal_values(seeds[6], (QUERY_HEADS * HEAD_DIM, MODEL_DIM), (QUERY_HEADS * HEAD_DIM // 4) ** -0.5, 0.125, ((0, 4), (1, 32)))
    post_gain = jnp.clip(1.0 + 0.18 * jax.random.normal(seeds[7], (MODEL_DIM,), jnp.float32), 0.099609375, 1.8984375).astype(jnp.bfloat16)
    routes_keys = jax.random.split(jax.random.fold_in(seeds[8], 1), TOKEN_TOTAL // TOK_DEV)
    routes_turns = jax.random.permutation(jax.random.fold_in(seeds[8], 3), TOKEN_TOTAL // TOK_DEV)
    routes = jax.vmap(lambda own, number: routed_block(jax.random.fold_in(seeds[8], 2), own, number, TOK_DEV, EXPERTS, TOP, CAP, 2))(routes_keys, routes_turns).reshape((TOKEN_TOTAL, TOP))
    route_gates = jnp.clip(jnp.exp(math.log(1.0) - 2.3025851 * jax.random.uniform(seeds[9], (TOKEN_TOTAL, TOP), jnp.float32) ** steps_of(seeds[9], (TOKEN_TOTAL, TOP), ((0, 2),), -0.2, 0.2)), 0.1, 1.0)
    w_gate = normal_values(seeds[10], (EXPERTS, MODEL_DIM, FF), MODEL_DIM ** -0.5, 0.09375, ((0, 64), (2, 4)))
    w_up = normal_values(seeds[11], (EXPERTS, MODEL_DIM, FF), MODEL_DIM ** -0.5, 0.09375, ((0, 64), (2, 4)))
    w_down = normal_values(seeds[12], (EXPERTS, FF, MODEL_DIM), (FF // 2) ** -0.5, 0.21875, ((0, 64), (1, 4)))
    return dict(tokens=tokens, attn_gain=attn_gain, w_query=w_query, q_gain=q_gain, cached_keys=cached_keys, prefix_values=prefix_values, output_weight=output_weight, post_gain=post_gain, routes=routes, route_gates=route_gates, w_gate=w_gate, w_up=w_up, w_down=w_down)


EPSILON = 1e-06
key_block_limit = 512

def attend_prefix(grouped_queries, cached_keys, prefix_values):
    key_count = cached_keys.shape[0]
    kv_count = cached_keys.shape[1] // HEAD_DIM
    block_width = min(key_block_limit, key_count)
    blocked_keys = cached_keys.reshape(key_count // block_width, block_width, kv_count, HEAD_DIM)
    blocked_values = prefix_values.reshape(key_count // block_width, block_width, kv_count, HEAD_DIM)
    query_rows = grouped_queries.astype(jnp.float32)
    row_count = grouped_queries.shape[1]
    start_state = (jnp.full((kv_count, row_count), -1e+30, jnp.float32), jnp.zeros((kv_count, row_count), jnp.float32), jnp.zeros((kv_count, row_count, HEAD_DIM), jnp.float32))

    def attend(running, key_values):
        row_peak, row_denominator, weighted_values = running
        key_block, value_block = key_values
        scores = jnp.einsum('jrd,bjd->jrb', query_rows, key_block.astype(jnp.float32), precision=lax.Precision.HIGHEST)
        new_peak = jnp.maximum(row_peak, lax.optimization_barrier(jnp.max(scores, axis=-1)))
        rescale = jnp.exp(row_peak - new_peak)
        weights = jnp.exp(scores - new_peak[..., None])
        row_denominator = row_denominator * rescale + lax.optimization_barrier(jnp.sum(weights, axis=-1))
        rounded = lax.optimization_barrier(weights.astype(jnp.bfloat16)).astype(jnp.float32)
        weighted_values = weighted_values * rescale[..., None] + jnp.einsum('jrb,bjd->jrd', rounded, value_block.astype(jnp.float32), precision=lax.Precision.HIGHEST)
        return ((new_peak, row_denominator, weighted_values), None)
    result, unused = lax.scan(attend, start_state, (blocked_keys, blocked_values))
    return result

def reference(tokens, attn_gain, w_query, q_gain, cached_keys, prefix_values, output_weight, post_gain, routes, route_gates, w_gate, w_up, w_down):
    group_width = QUERY_HEADS // KEY_VALUE_HEADS
    scaled = (tokens.astype(jnp.float32) * attn_gain.astype(jnp.float32)).astype(jnp.bfloat16)
    projected = jnp.dot(scaled, w_query, preferred_element_type=jnp.float32)
    per_head = projected.reshape(TOKEN_TOTAL, QUERY_HEADS, HEAD_DIM)
    inverse_rms = lax.rsqrt(lax.optimization_barrier(jnp.mean(per_head * per_head, axis=-1, keepdims=True)) + EPSILON)
    query_matrix = (per_head * inverse_rms * (q_gain.astype(jnp.float32) / jnp.sqrt(jnp.float32(HEAD_DIM)))).astype(jnp.bfloat16)
    grouped_queries = query_matrix.reshape(TOKEN_TOTAL, KEY_VALUE_HEADS, group_width, HEAD_DIM).transpose(1, 0, 2, 3).reshape(KEY_VALUE_HEADS, TOKEN_TOTAL * group_width, HEAD_DIM)
    row_peak, row_denominator, weighted_values = attend_prefix(grouped_queries, cached_keys, prefix_values)
    attended_rows = (weighted_values / row_denominator[..., None]).astype(jnp.bfloat16).reshape(KEY_VALUE_HEADS, TOKEN_TOTAL, group_width, HEAD_DIM)
    output_weights = output_weight.reshape(KEY_VALUE_HEADS, group_width, HEAD_DIM, MODEL_DIM)
    attn_proj = jnp.einsum('jtgd,jgdo->to', attended_rows.astype(jnp.float32), output_weights.astype(jnp.float32), precision=lax.Precision.HIGHEST)
    after_attn = (tokens.astype(jnp.float32) + attn_proj).astype(jnp.bfloat16)
    wide_rows = after_attn.astype(jnp.float32)
    row_mean = lax.optimization_barrier(jnp.mean(wide_rows * wide_rows, axis=-1, keepdims=True))
    normed = (wide_rows * lax.rsqrt(row_mean + EPSILON) * post_gain.astype(jnp.float32)).astype(jnp.bfloat16)
    flat_routes = routes.reshape(-1).astype(jnp.int32)
    assign_count = flat_routes.shape[0]
    order = jnp.argsort(flat_routes, stable=True).astype(jnp.int32)
    sorted_tokens = (order // TOP).astype(jnp.int32)
    sorted_gates = route_gates.reshape(-1)[order]
    expert_ids = jnp.arange(EXPERTS, dtype=jnp.int32)
    per_expert = lax.optimization_barrier(jnp.sum((flat_routes[None, :] == expert_ids[:, None]).astype(jnp.int32), axis=1))
    starts = (jnp.cumsum(per_expert) - per_expert).astype(jnp.int32)
    most_rows = min(TOKEN_TOTAL, EXPERTS * CAP)
    offsets = jnp.arange(most_rows, dtype=jnp.int32)

    def one_expert(mixture, expert_items):
        gate_matrix, up_matrix, down_matrix, expert_index = expert_items
        positions = starts[expert_index] + offsets
        valid = offsets < per_expert[expert_index]
        safe_positions = jnp.minimum(positions, assign_count - 1).astype(jnp.int32)
        token_index = sorted_tokens[safe_positions]
        chosen_rows = normed[token_index]
        gate_part = jnp.dot(chosen_rows, gate_matrix, preferred_element_type=jnp.float32)
        up_part = jnp.dot(chosen_rows, up_matrix, preferred_element_type=jnp.float32)
        hidden = (jax.nn.silu(gate_part) * up_part).astype(jnp.bfloat16)
        produced = jnp.dot(hidden, down_matrix, preferred_element_type=jnp.float32)
        factor = jnp.where(valid, sorted_gates[safe_positions], jnp.float32(0.0))
        mixture = mixture.at[token_index].add(factor[:, None] * produced)
        return (mixture, None)
    mixture, unused = lax.scan(one_expert, jnp.zeros((TOKEN_TOTAL, MODEL_DIM), jnp.float32), (w_gate, w_up, w_down, expert_ids))
    return (wide_rows + mixture).astype(jnp.bfloat16)
```

```python
import functools

import jax
import jax.numpy as jnp
from jax import lax
from jax.experimental import pallas as pl
from jax.experimental.pallas import tpu as pltpu
from jax.sharding import PartitionSpec as P

EPSILON = 1e-06
MIB = 1024 * 1024
NX, NZ, NH, NB = 4, 8, 4, 2
NE = NX * NZ
HEAD = 128
KEY_CHUNK = 512
MESH = pl.DeviceIdType.MESH
IN_VMEM = pl.BlockSpec(memory_space=pltpu.VMEM)
IN_ANY = pl.BlockSpec(memory_space=pl.ANY)
DMA = pltpu.SemaphoreType.DMA
NEAR_FIRST_Z = (1, 7, 2, 6, 3, 5, 4)
NEAR_FIRST_X = (1, 3, 2)


def remote(src, dst, send_sem, recv_sem, **where):
    return pltpu.make_async_remote_copy(
        src, dst, send_sem, recv_sem, device_id=where, device_id_type=MESH
    )


def here():
    expert = lax.axis_index("expert")
    return expert, expert // NX, lax.rem(expert, NX)


def signal(**where):
    pl.semaphore_signal(
        pltpu.get_barrier_semaphore(), inc=1, device_id=where, device_id_type=MESH
    )


def greet_lines(z, x):
    @pl.loop(1, NZ)
    def _(k):
        signal(expert=lax.rem(z + k, NZ) * NX + x)

    @pl.loop(1, NX)
    def _(k):
        signal(expert=z * NX + lax.rem(x + k, NX))


def greet_experts(expert):
    @pl.loop(1, NE)
    def _(k):
        signal(expert=lax.rem(expert + k, NE))


def gather_blocks(blocks, zs, zr, xs, xr):
    expert, z, x = here()

    def along_z(k, block, target):
        return remote(
            blocks.at[block], blocks.at[block], zs.at[k], zr.at[k], expert=target * NX + x
        )

    def along_x(j, k, column, target):
        block = lax.rem(z + NZ - j, NZ) * NX + column
        return remote(
            blocks.at[block],
            blocks.at[block],
            xs.at[j * NX + k],
            xr.at[j * NX + k],
            expert=z * NX + target,
        )

    for k in NEAR_FIRST_Z:
        along_z(k, expert, lax.rem(z + k, NZ)).start()
    for k in NEAR_FIRST_X:
        along_x(0, k, x, lax.rem(x + k, NX)).start()
    for j in NEAR_FIRST_Z:
        source = lax.rem(z + NZ - j, NZ)
        along_z(j, source * NX + x, source).wait_recv()
        for k in NEAR_FIRST_X:
            along_x(j, k, x, lax.rem(x + k, NX)).start()
    for j in (0,) + NEAR_FIRST_Z:
        for k in NEAR_FIRST_X:
            column = lax.rem(x + NX - k, NX)
            along_x(j, k, column, column).wait_recv()
    for k in NEAR_FIRST_Z:
        along_z(k, expert, lax.rem(z + k, NZ)).wait_send()
    for j in (0,) + NEAR_FIRST_Z:
        for k in NEAR_FIRST_X:
            along_x(j, k, x, lax.rem(x + k, NX)).wait_send()


def project_kernel(
    tokens, gain, w_query, q_gain, queries,
    scaled, weights, partial, arrived,
    ts, tr, ws, wr, ps, pr, zs, zr, xs, xr,
):
    expert, z, x = here()
    greet_lines(z, x)
    pl.semaphore_wait(pltpu.get_barrier_semaphore(), NZ + NX - 2)
    width = w_query.shape[1] // NX

    def columns(owner):
        return pl.ds(pl.multiple_of(owner * width, width), width)

    def weight_copy(k, owner, source):
        return remote(
            w_query.at[:, columns(owner)], weights.at[source], ws.at[k], wr.at[k],
            expert=z * NX + owner,
        )

    def token_copy(k, target, source):
        return remote(
            scaled.at[source], scaled.at[source], ts.at[k], tr.at[k], expert=z * NX + target
        )

    for k in NEAR_FIRST_X:
        weight_copy(k, lax.rem(x + k, NX), x).start()
    scaled[x] = (tokens[...].astype(jnp.float32) * gain[...].astype(jnp.float32)).astype(
        jnp.bfloat16
    )
    for k in NEAR_FIRST_X:
        token_copy(k, lax.rem(x + k, NX), x).start()
    weights[x] = w_query[:, columns(x)]
    for k in NEAR_FIRST_X:
        source = lax.rem(x + NX - k, NX)
        token_copy(k, source, source).wait_recv()
        weight_copy(k, source, source).wait_recv()
    rows = tokens.shape[0]
    left = jnp.concatenate([scaled[i] for i in range(NX)], axis=1)
    right = weights[...].reshape(NX * tokens.shape[1], width)
    product = jnp.dot(left, right, preferred_element_type=jnp.float32)
    partial[...] = product.reshape(NZ, rows // NZ, width)

    def sum_copy(k, target, source):
        return remote(
            partial.at[target], arrived.at[source], ps.at[k], pr.at[k], expert=target * NX + x
        )

    for k in NEAR_FIRST_Z:
        sum_copy(k, lax.rem(z + k, NZ), z).start()
    arrived[z] = partial[z]
    for k in NEAR_FIRST_Z:
        source = lax.rem(z + NZ - k, NZ)
        sum_copy(k, source, source).wait_recv()
    total = arrived[0]
    for i in range(1, NZ):
        total = total + arrived[i]
    factor = q_gain[...].astype(jnp.float32) / jnp.sqrt(jnp.float32(HEAD))
    heads = []
    for h in range(width // HEAD):
        one = total[:, h * HEAD : (h + 1) * HEAD]
        mean = jnp.mean(one * one, axis=-1, keepdims=True)
        heads.append(one * lax.rsqrt(mean + EPSILON) * factor)
    queries[expert] = jnp.concatenate(heads, axis=0).astype(jnp.bfloat16)
    gather_blocks(queries, zs, zr, xs, xr)
    for k in NEAR_FIRST_X:
        weight_copy(k, lax.rem(x + k, NX), x).wait_send()
        token_copy(k, lax.rem(x + k, NX), x).wait_send()
    for k in NEAR_FIRST_Z:
        sum_copy(k, lax.rem(z + k, NZ), z).wait_send()


def attend_block(queries, keys, values, scores):
    rows, count = scores.shape
    top = None
    for start in range(0, count, KEY_CHUNK):
        part = lax.dot_general(
            queries,
            keys[start : start + KEY_CHUNK, :],
            (((1,), (1,)), ((), ())),
            preferred_element_type=jnp.float32,
        )
        scores[:, start : start + KEY_CHUNK] = part
        for i in range(0, KEY_CHUNK, 128):
            piece = part[:, i : i + 128]
            top = piece if top is None else jnp.maximum(top, piece)
    peak = jnp.max(top, axis=1, keepdims=True)
    total = jnp.zeros((rows, 128), jnp.float32)
    weighted = jnp.zeros((rows, HEAD), jnp.float32)
    for start in range(0, count, KEY_CHUNK):
        probs = jnp.exp(scores[:, start : start + KEY_CHUNK] - peak)
        for i in range(0, KEY_CHUNK, 128):
            total = total + probs[:, i : i + 128]
        weighted = weighted + jnp.dot(
            probs.astype(jnp.bfloat16),
            values[start : start + KEY_CHUNK, :],
            preferred_element_type=jnp.float32,
        )
    total = jnp.sum(total, axis=1, keepdims=True)
    return weighted / total, peak + jnp.log(total)


def attend_kernel(
    queries, keys, values, output_weight, tokens, after,
    scores, averages, logs, their_averages, their_logs, attended, partial, arrived,
    os, orr, ls, lr, zs, zr, xs, xr, hs, hr,
):
    expert, z, x = here()
    head = lax.axis_index("head")
    greet_experts(expert)

    @pl.loop(1, NH)
    def _(k):
        signal(head=lax.rem(head + k, NH))

    pl.semaphore_wait(pltpu.get_barrier_semaphore(), NE - 1 + NH - 1)
    block = queries.shape[1]

    def average_copy(target, source):
        return remote(
            averages.at[target], their_averages.at[source], os.at[target], orr.at[source],
            expert=target,
        )

    def log_copy(target, source):
        return remote(
            logs.at[target], their_logs.at[source], ls.at[target], lr.at[source], expert=target
        )

    @pl.loop(0, NE // 2)
    def _(step):
        pair = lax.rem(expert // 2 + step, NE // 2) * 2
        rows = queries[pl.ds(pair, 2)].reshape(2 * block, HEAD)
        average, log_total = attend_block(rows, keys, values, scores)
        averages[pl.ds(pair, 2)] = average.astype(jnp.bfloat16).reshape(2, block, HEAD)
        wide = jnp.broadcast_to(log_total, (2 * block, 128))
        for i in range(2):
            logs[pair + i] = wide[i * block : (i + 1) * block].T[:8]
        for i in range(2):
            @pl.when(pair + i != expert)
            def _():
                average_copy(pair + i, expert).start()
                log_copy(pair + i, expert).start()

    their_averages[expert] = averages[expert]
    their_logs[expert] = logs[expert]

    @pl.loop(1, NE)
    def _(k):
        source = lax.rem(expert + NE - k, NE)
        log_copy(source, source).wait_recv()
        average_copy(source, source).wait_recv()

    each = their_logs[:, 0, :].T
    share = jnp.exp(each - jnp.max(each, axis=1, keepdims=True))
    share = share / jnp.sum(share, axis=1, keepdims=True)
    total = jnp.zeros((block, HEAD), jnp.float32)
    for i in range(NE):
        total = total + share[:, i : i + 1] * their_averages[i].astype(jnp.float32)
    attended[expert] = total.astype(jnp.bfloat16)
    gather_blocks(attended, zs, zr, xs, xr)

    heads_here = block // (tokens.shape[0] // NZ)
    span = block // heads_here
    everything = attended[...].reshape(NZ, NX, heads_here, span, HEAD)
    left = jnp.concatenate(
        [
            everything[:, i, j].reshape(NZ * span, HEAD)
            for i in range(NX)
            for j in range(heads_here)
        ],
        axis=1,
    )
    product = jnp.dot(left, output_weight[...], preferred_element_type=jnp.float32)
    quarter = tokens.shape[0] // NH
    partial[...] = product.reshape(NH, quarter, product.shape[1])

    def sum_copy(k, target, source):
        return remote(
            partial.at[target], arrived.at[source], hs.at[k], hr.at[k], head=target
        )

    for k in (1, 3, 2):
        sum_copy(k, lax.rem(head + k, NH), head).start()
    arrived[head] = partial[head]
    for k in (1, 3, 2):
        source = lax.rem(head + NH - k, NH)
        sum_copy(k, source, source).wait_recv()
    summed = arrived[0]
    for i in range(1, NH):
        summed = summed + arrived[i]
    mine = tokens[pl.ds(pl.multiple_of(head * quarter, quarter), quarter), :]
    after[...] = (mine.astype(jnp.float32) + summed).astype(jnp.bfloat16)

    @pl.loop(1, NE)
    def _(k):
        target = lax.rem(expert + k, NE)
        log_copy(target, expert).wait_send()
        average_copy(target, expert).wait_send()

    for k in (1, 3, 2):
        sum_copy(k, lax.rem(head + k, NH), head).wait_send()


def slot_matrix(routes, gates, experts, group):
    top, count = routes.shape
    names = lax.broadcasted_iota(jnp.int32, (experts, count), 0)
    chosen = jnp.zeros((experts, count), jnp.float32)
    gate = jnp.zeros((experts, count), jnp.float32)
    for k in range(top):
        hit = names == routes[k : k + 1, :]
        chosen = chosen + hit.astype(jnp.float32)
        gate = gate + jnp.where(hit, gates[k : k + 1, :], 0.0)
    earlier = lax.broadcasted_iota(jnp.int32, (count, count), 0)
    later = lax.broadcasted_iota(jnp.int32, (count, count), 1)
    before = ((earlier < later) & (earlier // group == later // group)).astype(jnp.bfloat16)
    rank = jnp.dot(chosen.astype(jnp.bfloat16), before, preferred_element_type=jnp.float32)
    place = chosen * (rank + 1.0)
    slots = 2 * (count // group)
    shape = (experts, slots, count)
    slot = lax.broadcasted_iota(jnp.int32, shape, 1)
    token = lax.broadcasted_iota(jnp.int32, shape, 2)
    wanted = (slot % 2 + 1).astype(jnp.float32)
    hits = (place[:, None, :] == wanted) & (token // group == slot // 2)
    places = hits.astype(jnp.float32)
    return places, places * gate[:, None, :]


def expert_kernel(
    after, routes, gates, post_gain, w_gate, w_up, w_down, out,
    gate_v, up_v, down_v, outgoing, stage, rows_all, normed, product, parts, back, returned,
    wsem, es, er, fs, fr, gs, gr, bs, br, ys, yr,
):
    expert, z, x = here()
    head = lax.axis_index("head")
    core = lax.axis_index("batch")
    load_gate = pltpu.make_async_copy(w_gate, gate_v, wsem.at[0])
    load_up = pltpu.make_async_copy(w_up, up_v, wsem.at[1])
    load_down = pltpu.make_async_copy(w_down, down_v, wsem.at[2])
    load_gate.start()
    load_up.start()
    load_down.start()
    greet_experts(expert)
    others = [(i, j) for j in range(NB) for i in range(NH) if (i, j) != (0, 0)]
    for i, j in others:
        signal(head=lax.rem(head + i, NH), batch=lax.rem(core + j, NB))
    pl.semaphore_wait(pltpu.get_barrier_semaphore(), NE - 1 + len(others))

    count, width = after.shape
    experts = NE * NB
    slots = rows_all.shape[3]
    places, weights = slot_matrix(routes[...], gates[...], experts, 8)
    picked = jnp.dot(
        places.reshape(experts * slots, count).astype(jnp.bfloat16),
        after[...],
        preferred_element_type=jnp.float32,
    ).astype(jnp.bfloat16)
    outgoing[...] = picked.reshape(NE, NB * slots, width)

    def out_copy(target, source):
        return remote(
            outgoing.at[target], stage.at[source], es.at[target], er.at[source], expert=target
        )

    @pl.loop(1, NE)
    def _(k):
        out_copy(lax.rem(expert + k, NE), expert).start()

    stage[expert] = outgoing[expert]
    groups = parts.shape[0]
    per_group = NE // groups
    own_group = expert // per_group

    def target_of(i, j):
        return lax.rem(head + i, NH), lax.rem(core + j, NB)

    def source_of(i, j):
        return lax.rem(head + NH - i, NH), lax.rem(core + NB - j, NB)

    def forward(g, i, j, to_head, to_core, from_head, from_core):
        return remote(
            stage.at[pl.ds(g * per_group, per_group), pl.ds(pl.multiple_of(to_core * slots, slots), slots)],
            rows_all.at[from_head, from_core, pl.ds(g * per_group, per_group)],
            fs.at[g, i * NB + j],
            fr.at[g, i * NB + j],
            head=to_head,
            batch=to_core,
        )

    @pl.loop(0, groups)
    def _(step):
        g = lax.rem(own_group + groups - step, groups)

        @pl.loop(0, per_group)
        def _(k):
            source = g * per_group + k

            @pl.when(source != expert)
            def _():
                out_copy(source, source).wait_recv()

        for i, j in others:
            to_head, to_core = target_of(i, j)
            forward(g, i, j, to_head, to_core, head, core).start()
        rows_all[head, core, pl.ds(g * per_group, per_group)] = stage[
            pl.ds(g * per_group, per_group), pl.ds(pl.multiple_of(core * slots, slots), slots)
        ]

    @pl.loop(0, groups)
    def _(step):
        g = lax.rem(own_group + groups - step, groups)
        for i, j in others:
            from_head, from_core = source_of(i, j)
            forward(g, i, j, from_head, from_core, from_head, from_core).wait_recv()

    held = NH * NB * slots
    square = jnp.zeros((held, width), jnp.float32)
    for e in range(NE):
        wide = rows_all[:, :, e].reshape(held, width).astype(jnp.float32)
        square = square + wide * wide
    mean = jnp.sum(square, axis=1, keepdims=True) * (1.0 / (NE * width))
    scale = lax.rsqrt(mean + EPSILON)
    for e in range(NE):
        wide = rows_all[:, :, e].reshape(held, width).astype(jnp.float32)
        normed[:, e * width : (e + 1) * width] = (
            wide * scale * post_gain[e : e + 1, :].astype(jnp.float32)
        ).astype(jnp.bfloat16)
    load_gate.wait()
    load_up.wait()
    gate_part = jnp.dot(normed[...], gate_v[...], preferred_element_type=jnp.float32)
    up_part = jnp.dot(normed[...], up_v[...], preferred_element_type=jnp.float32)
    hidden = (gate_part / (1.0 + jnp.exp(-gate_part)) * up_part).astype(jnp.bfloat16)
    load_down.wait()
    span = parts.shape[-1]

    def part_copy(g, i, j, to_head, to_core, from_head, from_core):
        return remote(
            product.at[g, to_head, to_core],
            parts.at[g, from_head, from_core],
            gs.at[g, i * NB + j],
            gr.at[g, i * NB + j],
            head=to_head,
            batch=to_core,
        )

    for g in range(groups):
        made = jnp.dot(
            hidden, down_v[:, g * span : (g + 1) * span], preferred_element_type=jnp.float32
        )
        product[g] = made.astype(jnp.bfloat16).reshape(NH, NB, slots, span)
        for i, j in others:
            to_head, to_core = target_of(i, j)
            part_copy(g, i, j, to_head, to_core, head, core).start()
        parts[g, head, core] = product[g, head, core]

    def back_copy(target, source):
        return remote(
            back.at[target], returned.at[source], bs.at[target], br.at[source], expert=target
        )

    for g in range(groups):
        for i, j in others:
            from_head, from_core = source_of(i, j)
            part_copy(g, i, j, from_head, from_core, from_head, from_core).wait_recv()
        total = parts[g, 0].astype(jnp.float32)
        for i in range(1, NH):
            total = total + parts[g, i].astype(jnp.float32)
        total = total.reshape(NB * slots, span).astype(jnp.bfloat16)
        for k in range(per_group):
            back[g * per_group + k] = total[:, k * width : (k + 1) * width]

        @pl.loop(0, per_group)
        def _(k):
            target = g * per_group + k

            @pl.when(target != expert)
            def _():
                back_copy(target, expert).start()

    returned[expert] = back[expert]

    @pl.loop(1, NE)
    def _(k):
        source = lax.rem(expert + NE - k, NE)
        back_copy(source, source).wait_recv()

    flat = weights.reshape(experts * slots, count)
    high = flat.astype(jnp.bfloat16)
    low = (flat - high.astype(jnp.float32)).astype(jnp.bfloat16)
    both = lax.dot_general(
        jnp.concatenate([high, low], axis=1),
        returned[...].reshape(experts * slots, width),
        (((0,), (0,)), ((), ())),
        preferred_element_type=jnp.float32,
    )
    mixture = both[:count] + both[count:]

    def rows_of(owner):
        return pl.ds(pl.multiple_of(owner * count, count), count)

    out[rows_of(head), :] = (after[...].astype(jnp.float32) + mixture).astype(jnp.bfloat16)

    def final_copy(k, target, source):
        return remote(
            out.at[rows_of(source)], out.at[rows_of(source)], ys.at[k], yr.at[k], head=target
        )

    for k in (1, 3, 2):
        final_copy(k, lax.rem(head + k, NH), head).start()
    for k in (1, 3, 2):
        source = lax.rem(head + NH - k, NH)
        final_copy(k, source, source).wait_recv()

    @pl.loop(1, NE)
    def _(k):
        target = lax.rem(expert + k, NE)
        out_copy(target, expert).wait_send()
        back_copy(target, expert).wait_send()

    @pl.loop(0, groups)
    def _(g):
        for i, j in others:
            to_head, to_core = target_of(i, j)
            forward(g, i, j, to_head, to_core, head, core).wait_send()
            part_copy(g, i, j, to_head, to_core, head, core).wait_send()

    for k in (1, 3, 2):
        final_copy(k, lax.rem(head + k, NH), head).wait_send()


def params(collective_id, mib):
    return pltpu.CompilerParams(
        collective_id=collective_id, has_side_effects=True, vmem_limit_bytes=mib * MIB
    )


def on_device(
    tokens, attn_gain, w_query, q_gain, cached_keys, prefix_values, output_weight,
    post_gain, routes, route_gates, w_gate, w_up, w_down,
):
    rows, width = tokens.shape
    block = rows * w_query.shape[1] // HEAD // NE
    bf16, f32 = jnp.bfloat16, jnp.float32
    queries = pl.pallas_call(
        project_kernel,
        out_shape=jax.ShapeDtypeStruct((NE, block, HEAD), bf16),
        in_specs=[IN_VMEM] * 4,
        out_specs=IN_VMEM,
        scratch_shapes=[
            pltpu.VMEM((NX, rows, width), bf16),
            pltpu.VMEM((NX, width, w_query.shape[1] // NX), bf16),
            pltpu.VMEM((NZ, rows // NZ, w_query.shape[1] // NX), f32),
            pltpu.VMEM((NZ, rows // NZ, w_query.shape[1] // NX), f32),
            DMA((NX,)), DMA((NX,)), DMA((NX,)), DMA((NX,)),
            DMA((NZ,)), DMA((NZ,)),
            DMA((NZ,)), DMA((NZ,)), DMA((NZ * NX,)), DMA((NZ * NX,)),
        ],
        compiler_params=params(1, 24),
        name="project_queries",
    )(tokens, attn_gain[None, :], w_query, q_gain[None, :])

    keys = cached_keys.shape[0]
    quarter = rows // NH
    after = pl.pallas_call(
        attend_kernel,
        out_shape=jax.ShapeDtypeStruct((quarter, width), bf16),
        in_specs=[IN_VMEM] * 5,
        out_specs=IN_VMEM,
        scratch_shapes=[
            pltpu.VMEM((2 * block, keys), f32),
            pltpu.VMEM((NE, block, HEAD), bf16),
            pltpu.VMEM((NE, 8, block), f32),
            pltpu.VMEM((NE, block, HEAD), bf16),
            pltpu.VMEM((NE, 8, block), f32),
            pltpu.VMEM((NE, block, HEAD), bf16),
            pltpu.VMEM((NH, quarter, width), f32),
            pltpu.VMEM((NH, quarter, width), f32),
            DMA((NE,)), DMA((NE,)), DMA((NE,)), DMA((NE,)),
            DMA((NZ,)), DMA((NZ,)), DMA((NZ * NX,)), DMA((NZ * NX,)),
            DMA((NH,)), DMA((NH,)),
        ],
        compiler_params=params(2, 40),
        name="attend_prefix",
    )(queries, cached_keys, prefix_values, output_weight, tokens)

    start = lax.axis_index("head") * quarter
    my_routes = lax.dynamic_slice_in_dim(routes, start, quarter, 0).T
    my_gates = lax.dynamic_slice_in_dim(route_gates, start, quarter, 0).T
    model, ff = w_gate.shape[1:]
    slots = 2 * quarter // 8
    groups = 4
    return pl.pallas_call(
        expert_kernel,
        out_shape=jax.ShapeDtypeStruct((rows, width), bf16),
        in_specs=[IN_VMEM] * 4 + [IN_ANY] * 3,
        out_specs=IN_VMEM,
        scratch_shapes=[
            pltpu.VMEM((model, ff), bf16),
            pltpu.VMEM((model, ff), bf16),
            pltpu.VMEM((ff, model), bf16),
            pltpu.VMEM((NE, NB * slots, width), bf16),
            pltpu.VMEM((NE, NB * slots, width), bf16),
            pltpu.VMEM((NH, NB, NE, slots, width), bf16),
            pltpu.VMEM((NH * NB * slots, model), bf16),
            pltpu.VMEM((groups, NH, NB, slots, model // groups), bf16),
            pltpu.VMEM((groups, NH, NB, slots, model // groups), bf16),
            pltpu.VMEM((NE, NB * slots, width), bf16),
            pltpu.VMEM((NE, NB * slots, width), bf16),
            DMA((3,)), DMA((NE,)), DMA((NE,)),
            DMA((groups, NH * NB)), DMA((groups, NH * NB)),
            DMA((groups, NH * NB)), DMA((groups, NH * NB)),
            DMA((NE,)), DMA((NE,)), DMA((NH,)), DMA((NH,)),
        ],
        compiler_params=params(3, 40),
        name="routed_experts",
    )(
        after, my_routes, my_gates, post_gain.reshape(NE, width),
        w_gate[0], w_up[0], w_down[0],
    )


def solution(mesh):
    placed = (
        P("batch", "expert"),
        P("expert"),
        P("expert", "head"),
        P(),
        P("expert", "head"),
        P("expert", "head"),
        P("head", "expert"),
        P(),
        P("batch", None),
        P("batch", None),
        P(("expert", "batch"), None, "head"),
        P(("expert", "batch"), None, "head"),
        P(("expert", "batch"), "head", None),
    )
    return jax.shard_map(
        on_device, mesh=mesh, in_specs=placed, out_specs=P("batch", "expert"), check_vma=False
    )
```

```python
import functools

import jax
import jax.numpy as jnp
from jax import lax
from jax.experimental import pallas as pl
from jax.experimental.pallas import tpu as pltpu
from jax.sharding import PartitionSpec as P

EPSILON = 1e-06
MIB = 1024 * 1024
NX, NZ, NH, NB = 4, 8, 4, 2
NE = NX * NZ
HEAD = 128
KEY_CHUNK = 256
MESH = pl.DeviceIdType.MESH
IN_VMEM = pl.BlockSpec(memory_space=pltpu.VMEM)
IN_ANY = pl.BlockSpec(memory_space=pl.ANY)
DMA = pltpu.SemaphoreType.DMA
NEAR_FIRST_Z = (1, 7, 2, 6, 3, 5, 4)
NEAR_FIRST_X = (1, 3, 2)


def remote(src, dst, send_sem, recv_sem, **where):
    return pltpu.make_async_remote_copy(
        src, dst, send_sem, recv_sem, device_id=where, device_id_type=MESH
    )


def here():
    expert = lax.axis_index("expert")
    return expert, expert // NX, lax.rem(expert, NX)


def signal(**where):
    pl.semaphore_signal(
        pltpu.get_barrier_semaphore(), inc=1, device_id=where, device_id_type=MESH
    )


def greet_experts(expert):
    @pl.loop(1, NE)
    def _(k):
        signal(expert=lax.rem(expert + k, NE))


def slot_matrix(routes, gates, experts, group):
    top, count = routes.shape
    names = lax.broadcasted_iota(jnp.int32, (experts, count), 0)
    chosen = jnp.zeros((experts, count), jnp.float32)
    gate = jnp.zeros((experts, count), jnp.float32)
    for k in range(top):
        hit = names == routes[k : k + 1, :]
        chosen = chosen + hit.astype(jnp.float32)
        gate = gate + jnp.where(hit, gates[k : k + 1, :], 0.0)
    earlier = lax.broadcasted_iota(jnp.int32, (count, count), 0)
    later = lax.broadcasted_iota(jnp.int32, (count, count), 1)
    before = ((earlier < later) & (earlier // group == later // group)).astype(jnp.bfloat16)
    rank = jnp.dot(chosen.astype(jnp.bfloat16), before, preferred_element_type=jnp.float32)
    place = chosen * (rank + 1.0)
    slots = 2 * (count // group)
    shape = (experts, slots, count)
    slot = lax.broadcasted_iota(jnp.int32, shape, 1)
    token = lax.broadcasted_iota(jnp.int32, shape, 2)
    wanted = (slot % 2 + 1).astype(jnp.float32)
    hits = (place[:, None, :] == wanted) & (token // group == slot // 2)
    places = hits.astype(jnp.float32)
    return places, places * gate[:, None, :]


def transposed_softmax(queries, keys, values_t, scores):
    count, rows = scores.shape
    chunks = range(0, count, KEY_CHUNK)
    top = jnp.full((8, rows), -jnp.inf, jnp.float32)
    for start in chunks:
        part = lax.dot_general(
            keys[start : start + KEY_CHUNK, :],
            queries,
            (((1,), (1,)), ((), ())),
            preferred_element_type=jnp.float32,
        )
        scores[start : start + KEY_CHUNK, :] = part
        top = jnp.maximum(top, jnp.max(part.reshape(KEY_CHUNK // 8, 8, rows), axis=0))
    peak = jnp.max(top, axis=0, keepdims=True)
    total = jnp.zeros((8, rows), jnp.float32)
    weighted = jnp.zeros((HEAD, rows), jnp.float32)
    for start in chunks:
        probs = jnp.exp(scores[start : start + KEY_CHUNK, :] - peak)
        total = total + jnp.sum(probs.reshape(KEY_CHUNK // 8, 8, rows), axis=0)
        weighted = weighted + jnp.dot(
            values_t[:, start : start + KEY_CHUNK],
            probs.astype(jnp.bfloat16),
            preferred_element_type=jnp.float32,
        )
    total = jnp.sum(total, axis=0, keepdims=True)
    return weighted / total, peak + jnp.log(total)


def merged(averages, logs):
    top = logs[0]
    for one in logs[1:]:
        top = jnp.maximum(top, one)
    shares = [jnp.exp(one - top) for one in logs]
    total = shares[0]
    for one in shares[1:]:
        total = total + one
    inverse = 1.0 / total
    result = None
    for one, share in zip(averages, shares):
        term = one.astype(jnp.float32) * (share * inverse)[0:1]
        result = term if result is None else result + term
    return result, top + jnp.log(total)


def layer_kernel(
    tokens, gain, w_query, q_gain, keys_h, values_h, output_h, post_gain, routes, gates,
    w_gate, w_up, w_down, out,
    scaled, weights, partial, arrived, queries, keys, values, values_t, output_weight, scores,
    average_s, log_s, average_x, log_x, merged_s, mlog_s, merged_z, mlog_z, attended,
    part, part_r, after,
    places, mixing, gate_v, up_v, down_v, outgoing, stage, rows_all, normed, product, parts,
    back, returned, final_s, final_r,
    load, ts, tr, ws, wr, ps, pr, qs, qr, fqs, fqr,
    xas, xar, xls, xlr, zas, zar, zls, zlr, ms, mr, fms, fmr, hs, hr,
    es, er, fs, fr, gs, gr, bs, br, ys, yr,
):
    expert, z, x = here()
    head = lax.axis_index("head")
    core = lax.axis_index("batch")
    f32, bf16 = jnp.float32, jnp.bfloat16
    width = w_query.shape[1] // NX
    rows, features = tokens.shape
    block = queries.shape[1]
    span = rows // NZ
    heads_here = width // HEAD
    sub = span // NH
    count = NZ * sub
    others = [(i, j) for j in range(NB) for i in range(NH) if (i, j) != (0, 0)]

    def columns(owner):
        return pl.ds(pl.multiple_of(owner * width, width), width)

    own_weights = pltpu.make_async_copy(w_query.at[:, columns(x)], weights.at[x], load.at[0])
    own_weights.start()
    load_keys = pltpu.make_async_copy(keys_h, keys, load.at[1])
    load_values = pltpu.make_async_copy(values_h, values, load.at[2])
    load_output = pltpu.make_async_copy(output_h, output_weight, load.at[3])
    load_gate = pltpu.make_async_copy(w_gate, gate_v, load.at[4])
    load_up = pltpu.make_async_copy(w_up, up_v, load.at[5])
    load_down = pltpu.make_async_copy(w_down, down_v, load.at[6])

    @pl.loop(1, NE)
    def _(k):
        signal(expert=lax.rem(expert + k, NE))

    for i, j in others:
        signal(head=lax.rem(head + i, NH), batch=lax.rem(core + j, NB))
    scaled[x] = (tokens[...].astype(f32) * gain[...].astype(f32)).astype(bf16)
    pl.semaphore_wait(pltpu.get_barrier_semaphore(), NE - 1 + len(others))

    def weight_copy(k, owner, source):
        return remote(
            w_query.at[:, columns(owner)], weights.at[source], ws.at[k], wr.at[k],
            expert=z * NX + owner,
        )

    def token_copy(k, target, source):
        return remote(
            scaled.at[source], scaled.at[source], ts.at[k], tr.at[k], expert=z * NX + target
        )

    def sum_copy(k, target, source):
        return remote(
            partial.at[target], arrived.at[source], ps.at[k], pr.at[k], expert=target * NX + x
        )

    for k in NEAR_FIRST_X:
        target = lax.rem(x + k, NX)
        token_copy(k, target, x).start()
        weight_copy(k, target, x).start()
    load_keys.start()
    load_values.start()
    load_output.start()
    slots = 2 * count // 8
    experts = NE * NB
    chosen, weighted = slot_matrix(routes[...], gates[...], experts, 8)
    places[...] = chosen.reshape(experts * slots, count).astype(bf16)
    flat = weighted.reshape(experts * slots, count)
    high = flat.astype(bf16)
    mixing[...] = jnp.concatenate([high, (flat - high.astype(f32)).astype(bf16)], axis=1)
    own_weights.wait()
    for k in NEAR_FIRST_X:
        source = lax.rem(x + NX - k, NX)
        token_copy(k, source, source).wait_recv()
        weight_copy(k, source, source).wait_recv()
    left = jnp.concatenate([scaled[i] for i in range(NX)], axis=1)
    right = weights[...].reshape(NX * features, width)
    partial[...] = jnp.dot(left, right, preferred_element_type=f32).reshape(NZ, span, width)
    for k in NEAR_FIRST_Z:
        sum_copy(k, lax.rem(z + k, NZ), z).start()
    arrived[z] = partial[z]
    load_gate.start()
    load_up.start()
    load_down.start()
    load_values.wait()
    for i in range(0, values.shape[0], 128):
        values_t[:, i : i + 128] = values[i : i + 128, :].astype(f32).T.astype(bf16)
    for k in NEAR_FIRST_Z:
        source = lax.rem(z + NZ - k, NZ)
        sum_copy(k, source, source).wait_recv()
    total = arrived[0]
    for i in range(1, NZ):
        total = total + arrived[i]
    factor = q_gain[...].astype(f32) / jnp.sqrt(f32(HEAD))
    heads = []
    for h in range(heads_here):
        one = total[:, h * HEAD : (h + 1) * HEAD]
        mean = jnp.mean(one * one, axis=-1, keepdims=True)
        heads.append(one * lax.rsqrt(mean + EPSILON) * factor)
    queries[expert] = jnp.concatenate(heads, axis=0).astype(bf16)

    def query_z(target, source):
        return remote(
            queries.at[source * NX + x], queries.at[source * NX + x],
            qs.at[target], qr.at[source], expert=target * NX + x,
        )

    def query_x(r, k, target, column):
        return remote(
            queries.at[r * NX + column], queries.at[r * NX + column],
            fqs.at[r * NX + k], fqr.at[r * NX + k], expert=z * NX + target,
        )

    def forward_queries(r):
        @pl.when(r != z)
        def _():
            query_z(r, r).wait_recv()

        for k in NEAR_FIRST_X:
            query_x(r, k, lax.rem(x + k, NX), x).start()

    for k in NEAR_FIRST_Z:
        query_z(lax.rem(z + k, NZ), z).start()
    load_keys.wait()
    load_output.wait()
    ahead = 2
    for r in range(ahead):
        forward_queries(r)

    def average_copy(r, k, target, source):
        return remote(
            average_s.at[r, target], average_x.at[r, source],
            xas.at[r * NX + k], xar.at[r * NX + k], expert=z * NX + target,
        )

    def log_copy(r, k, target, source):
        return remote(
            log_s.at[r, target], log_x.at[r, source],
            xls.at[r * NX + k], xlr.at[r * NX + k], expert=z * NX + target,
        )

    def merged_copy(target, source):
        return remote(
            merged_s.at[target], merged_z.at[source], zas.at[target], zar.at[source],
            expert=target * NX + x,
        )

    def mlog_copy(target, source):
        return remote(
            mlog_s.at[target], mlog_z.at[source], zls.at[target], zlr.at[source],
            expert=target * NX + x,
        )

    def attended_z(target, source):
        return remote(
            attended.at[source * NX + x], attended.at[source * NX + x],
            ms.at[target], mr.at[source], expert=target * NX + x,
        )

    def attended_x(r, k, target, column):
        return remote(
            attended.at[r * NX + column], attended.at[r * NX + column],
            fms.at[r * NX + k], fmr.at[r * NX + k], expert=z * NX + target,
        )

    def head_copy(r, k, target, source):
        return remote(
            part.at[r, target], part_r.at[source, r],
            hs.at[r * NH + k], hr.at[r * NH + k], head=target,
        )

    def attend(r):
        for k in NEAR_FIRST_X:
            column = lax.rem(x + NX - k, NX)
            query_x(r, k, column, column).wait_recv()
        here_rows = queries[pl.ds(r * NX, NX)].reshape(NX * block, HEAD)
        average, log_total = transposed_softmax(here_rows, keys, values_t, scores)
        average = average.astype(bf16)
        log_total = jnp.broadcast_to(log_total, (8, NX * block))
        for i in range(NX):
            average_s[r, i] = average[:, i * block : (i + 1) * block]
            log_s[r, i] = log_total[:, i * block : (i + 1) * block]
        for k in NEAR_FIRST_X:
            target = lax.rem(x + k, NX)
            log_copy(r, k, target, x).start()
            average_copy(r, k, target, x).start()
        average_x[r, x] = average_s[r, x]
        log_x[r, x] = log_s[r, x]

    def merge_x(r):
        for k in NEAR_FIRST_X:
            source = lax.rem(x + NX - k, NX)
            log_copy(r, k, source, source).wait_recv()
            average_copy(r, k, source, source).wait_recv()
        average, log_total = merged(
            [average_x[r, i] for i in range(NX)], [log_x[r, i] for i in range(NX)]
        )
        average = average.astype(bf16)

        @pl.when(r == z)
        def _():
            merged_z[z] = average
            mlog_z[z] = log_total

        @pl.when(r != z)
        def _():
            merged_s[r] = average
            mlog_s[r] = log_total
            mlog_copy(r, z).start()
            merged_copy(r, z).start()

    def merge_z(r):
        @pl.when(r == z)
        def _():
            @pl.loop(1, NZ)
            def _(k):
                source = lax.rem(z + k, NZ)
                mlog_copy(source, source).wait_recv()
                merged_copy(source, source).wait_recv()

            average, _ = merged(
                [merged_z[i] for i in range(NZ)], [mlog_z[i] for i in range(NZ)]
            )
            attended[expert] = average.T.astype(bf16)
            for k in NEAR_FIRST_Z:
                attended_z(lax.rem(z + k, NZ), z).start()

    def forward_attended(r):
        @pl.when(r != z)
        def _():
            attended_z(r, r).wait_recv()

        for k in NEAR_FIRST_X:
            attended_x(r, k, lax.rem(x + k, NX), x).start()

    def project(r):
        for k in NEAR_FIRST_X:
            column = lax.rem(x + NX - k, NX)
            attended_x(r, k, column, column).wait_recv()
        left = jnp.concatenate(
            [
                attended[r * NX + i, j * span : (j + 1) * span, :]
                for i in range(NX)
                for j in range(heads_here)
            ],
            axis=1,
        )
        made = jnp.dot(left, output_weight[...], preferred_element_type=f32)
        part[r] = made.reshape(NH, sub, features)
        for k in (1, 3, 2):
            head_copy(r, k, lax.rem(head + k, NH), head).start()
        part_r[head, r] = part[r, head]

    @pl.loop(0, NZ + 4)
    def _(step):
        @pl.when(step + ahead < NZ)
        def _():
            forward_queries(step + ahead)

        @pl.when(step < NZ)
        def _():
            attend(step)

        for offset, stage_of in ((4, project), (3, forward_attended), (2, merge_z), (1, merge_x)):
            @pl.when((step >= offset) & (step < NZ + offset))
            def _():
                stage_of(step - offset)

    for r in range(NZ):
        for k in (1, 3, 2):
            source = lax.rem(head + NH - k, NH)
            head_copy(r, k, source, source).wait_recv()
    for r in range(NZ):
        summed = part_r[0, r]
        for i in range(1, NH):
            summed = summed + part_r[i, r]
        after[r * sub : (r + 1) * sub, :] = summed
    resid = tokens[...].astype(f32).reshape(NZ, NH, sub, features)
    mine = jnp.zeros((NZ, sub, features), f32)
    for i in range(NH):
        mine = jnp.where(head == i, resid[:, i], mine)
    stream = (mine.reshape(count, features) + after[...]).astype(bf16)

    def out_copy(target, source):
        return remote(
            outgoing.at[target], stage.at[source], es.at[target], er.at[source], expert=target
        )

    picked = jnp.dot(places[...], stream, preferred_element_type=f32).astype(bf16)
    outgoing[...] = picked.reshape(NE, NB * slots, features)

    @pl.loop(1, NE)
    def _(k):
        out_copy(lax.rem(expert + k, NE), expert).start()

    stage[expert] = outgoing[expert]
    groups = parts.shape[0]
    per_group = NE // groups
    own_group = expert // per_group

    def target_of(i, j):
        return lax.rem(head + i, NH), lax.rem(core + j, NB)

    def source_of(i, j):
        return lax.rem(head + NH - i, NH), lax.rem(core + NB - j, NB)

    def half(owner):
        return pl.ds(pl.multiple_of(owner * slots, slots), slots)

    def forward(g, i, j, to_head, to_core, from_head, from_core):
        return remote(
            stage.at[pl.ds(g * per_group, per_group), half(to_core)],
            rows_all.at[from_head, from_core, pl.ds(g * per_group, per_group)],
            fs.at[g, i * NB + j],
            fr.at[g, i * NB + j],
            head=to_head,
            batch=to_core,
        )

    @pl.loop(0, groups)
    def _(step):
        g = lax.rem(own_group + groups - step, groups)

        @pl.loop(0, per_group)
        def _(k):
            source = g * per_group + k

            @pl.when(source != expert)
            def _():
                out_copy(source, source).wait_recv()

        for i, j in others:
            to_head, to_core = target_of(i, j)
            forward(g, i, j, to_head, to_core, head, core).start()
        rows_all[head, core, pl.ds(g * per_group, per_group)] = stage[
            pl.ds(g * per_group, per_group), half(core)
        ]

    load_gate.wait()
    load_up.wait()
    load_down.wait()

    @pl.loop(0, groups)
    def _(step):
        g = lax.rem(own_group + groups - step, groups)
        for i, j in others:
            from_head, from_core = source_of(i, j)
            forward(g, i, j, from_head, from_core, from_head, from_core).wait_recv()

    held = NH * NB * slots
    square = jnp.zeros((held, features), f32)
    for e in range(NE):
        wide = rows_all[:, :, e].reshape(held, features).astype(f32)
        square = square + wide * wide
    mean = jnp.sum(square, axis=1, keepdims=True) * (1.0 / (NE * features))
    scale = lax.rsqrt(mean + EPSILON)
    for e in range(NE):
        wide = rows_all[:, :, e].reshape(held, features).astype(f32)
        normed[:, e * features : (e + 1) * features] = (
            wide * scale * post_gain[e : e + 1, :].astype(f32)
        ).astype(bf16)
    gate_part = jnp.dot(normed[...], gate_v[...], preferred_element_type=f32)
    up_part = jnp.dot(normed[...], up_v[...], preferred_element_type=f32)
    hidden = (gate_part / (1.0 + jnp.exp(-gate_part)) * up_part).astype(bf16)
    reach = parts.shape[-1]

    def part_copy(g, i, j, to_head, to_core, from_head, from_core):
        return remote(
            product.at[g, to_head, to_core],
            parts.at[g, from_head, from_core],
            gs.at[g, i * NB + j],
            gr.at[g, i * NB + j],
            head=to_head,
            batch=to_core,
        )

    for g in range(groups):
        made = jnp.dot(hidden, down_v[:, g * reach : (g + 1) * reach], preferred_element_type=f32)
        product[g] = made.astype(bf16).reshape(NH, NB, slots, reach)
        for i, j in others:
            to_head, to_core = target_of(i, j)
            part_copy(g, i, j, to_head, to_core, head, core).start()
        parts[g, head, core] = product[g, head, core]

    def back_copy(target, source):
        return remote(
            back.at[target], returned.at[source], bs.at[target], br.at[source], expert=target
        )

    for g in range(groups):
        for i, j in others:
            from_head, from_core = source_of(i, j)
            part_copy(g, i, j, from_head, from_core, from_head, from_core).wait_recv()
        total = parts[g, 0].astype(f32)
        for i in range(1, NH):
            total = total + parts[g, i].astype(f32)
        total = total.reshape(NB * slots, reach).astype(bf16)
        for k in range(per_group):
            back[g * per_group + k] = total[:, k * features : (k + 1) * features]

        @pl.loop(0, per_group)
        def _(k):
            target = g * per_group + k

            @pl.when(target != expert)
            def _():
                back_copy(target, expert).start()

    returned[expert] = back[expert]

    @pl.loop(1, NE)
    def _(k):
        source = lax.rem(expert + NE - k, NE)
        back_copy(source, source).wait_recv()

    both = lax.dot_general(
        mixing[...],
        returned[...].reshape(experts * slots, features),
        (((0,), (0,)), ((), ())),
        preferred_element_type=f32,
    )
    mixture = both[:count] + both[count:]
    final_s[...] = (stream.astype(f32) + mixture).astype(bf16)

    def final_copy(k, target, source):
        return remote(final_s, final_r.at[source], ys.at[k], yr.at[k], head=target)

    for k in (1, 3, 2):
        final_copy(k, lax.rem(head + k, NH), head).start()
    final_r[head] = final_s[...]
    for k in (1, 3, 2):
        source = lax.rem(head + NH - k, NH)
        final_copy(k, source, source).wait_recv()
    pieces = [final_r[i].astype(f32).reshape(NZ, sub, features) for i in range(NH)]
    out[...] = jnp.concatenate(
        [pieces[i][r] for r in range(NZ) for i in range(NH)], axis=0
    ).astype(bf16)

    for k in NEAR_FIRST_X:
        target = lax.rem(x + k, NX)
        token_copy(k, target, x).wait_send()
        weight_copy(k, target, x).wait_send()

        @pl.loop(0, NZ)
        def _(r):
            query_x(r, k, target, x).wait_send()
            average_copy(r, k, target, x).wait_send()
            log_copy(r, k, target, x).wait_send()
            attended_x(r, k, target, x).wait_send()

    @pl.loop(1, NZ)
    def _(k):
        target = lax.rem(z + k, NZ)
        sum_copy(k, target, z).wait_send()
        query_z(target, z).wait_send()
        merged_copy(target, z).wait_send()
        mlog_copy(target, z).wait_send()
        attended_z(target, z).wait_send()

    for k in (1, 3, 2):
        target = lax.rem(head + k, NH)
        final_copy(k, target, head).wait_send()

        @pl.loop(0, NZ)
        def _(r):
            head_copy(r, k, target, head).wait_send()

    @pl.loop(1, NE)
    def _(k):
        target = lax.rem(expert + k, NE)
        out_copy(target, expert).wait_send()
        back_copy(target, expert).wait_send()

    @pl.loop(0, groups)
    def _(g):
        for i, j in others:
            to_head, to_core = target_of(i, j)
            forward(g, i, j, to_head, to_core, head, core).wait_send()
            part_copy(g, i, j, to_head, to_core, head, core).wait_send()


def on_device(
    tokens, attn_gain, w_query, q_gain, cached_keys, prefix_values, output_weight,
    post_gain, routes, route_gates, w_gate, w_up, w_down,
):
    rows, features = tokens.shape
    width = w_query.shape[1] // NX
    block = rows * w_query.shape[1] // HEAD // NE
    bf16, f32 = jnp.bfloat16, jnp.float32
    keys = cached_keys.shape[0]
    span = rows // NZ
    sub = span // NH
    count = NZ * sub
    head = lax.axis_index("head")
    top = routes.shape[1]

    def mine(table):
        cut = lax.dynamic_index_in_dim(table.reshape(NZ, NH, sub, top), head, 1, False)
        return cut.reshape(count, top).T

    model, ff = w_gate.shape[1:]
    slots = 2 * count // 8
    groups = 4
    experts = NE * NB
    V = pltpu.VMEM
    return pl.pallas_call(
        layer_kernel,
        out_shape=jax.ShapeDtypeStruct((rows, features), bf16),
        in_specs=[IN_VMEM, IN_VMEM, IN_ANY, IN_VMEM] + [IN_ANY] * 3 + [IN_VMEM] * 3 + [IN_ANY] * 3,
        out_specs=IN_VMEM,
        scratch_shapes=[
            V((NX, rows, features), bf16),
            V((NX, features, width), bf16),
            V((NZ, span, width), f32),
            V((NZ, span, width), f32),
            V((NE, block, HEAD), bf16),
            V((keys, HEAD), bf16),
            V((keys, HEAD), bf16),
            V((HEAD, keys), bf16),
            V(output_weight.shape, bf16),
            V((keys, NX * block), f32),
            V((NZ, NX, HEAD, block), bf16),
            V((NZ, NX, 8, block), f32),
            V((NZ, NX, HEAD, block), bf16),
            V((NZ, NX, 8, block), f32),
            V((NZ, HEAD, block), bf16),
            V((NZ, 8, block), f32),
            V((NZ, HEAD, block), bf16),
            V((NZ, 8, block), f32),
            V((NE, block, HEAD), bf16),
            V((NZ, NH, sub, features), f32),
            V((NH, NZ, sub, features), f32),
            V((count, features), f32),
            V((experts * slots, count), bf16),
            V((experts * slots, 2 * count), bf16),
            V((model, ff), bf16),
            V((model, ff), bf16),
            V((ff, model), bf16),
            V((NE, NB * slots, features), bf16),
            V((NE, NB * slots, features), bf16),
            V((NH, NB, NE, slots, features), bf16),
            V((NH * NB * slots, model), bf16),
            V((groups, NH, NB, slots, model // groups), bf16),
            V((groups, NH, NB, slots, model // groups), bf16),
            V((NE, NB * slots, features), bf16),
            V((NE, NB * slots, features), bf16),
            V((count, features), bf16),
            V((NH, count, features), bf16),
            DMA((7,)),
            DMA((NX,)), DMA((NX,)), DMA((NX,)), DMA((NX,)),
            DMA((NZ,)), DMA((NZ,)),
            DMA((NZ,)), DMA((NZ,)), DMA((NE,)), DMA((NE,)),
            DMA((NE,)), DMA((NE,)), DMA((NE,)), DMA((NE,)),
            DMA((NZ,)), DMA((NZ,)), DMA((NZ,)), DMA((NZ,)),
            DMA((NZ,)), DMA((NZ,)), DMA((NE,)), DMA((NE,)),
            DMA((NZ * NH,)), DMA((NZ * NH,)),
            DMA((NE,)), DMA((NE,)),
            DMA((groups, NH * NB)), DMA((groups, NH * NB)),
            DMA((groups, NH * NB)), DMA((groups, NH * NB)),
            DMA((NE,)), DMA((NE,)), DMA((NH,)), DMA((NH,)),
        ],
        compiler_params=pltpu.CompilerParams(
            collective_id=1, has_side_effects=True, vmem_limit_bytes=56 * MIB
        ),
        name="scoring_layer",
    )(
        tokens, attn_gain[None, :], w_query, q_gain[None, :],
        cached_keys, prefix_values, output_weight,
        post_gain.reshape(NE, features), mine(routes), mine(route_gates),
        w_gate[0], w_up[0], w_down[0],
    )


def solution(mesh):
    placed = (
        P("batch", "expert"),
        P("expert"),
        P("expert", "head"),
        P(),
        P("expert", "head"),
        P("expert", "head"),
        P("head", "expert"),
        P(),
        P("batch", None),
        P("batch", None),
        P(("expert", "batch"), None, "head"),
        P(("expert", "batch"), None, "head"),
        P(("expert", "batch"), "head", None),
    )
    return jax.shard_map(
        on_device, mesh=mesh, in_specs=placed, out_specs=P("batch", "expert"), check_vma=False
    )
```

```python
import functools

import jax
import jax.numpy as jnp
from jax import lax
from jax.experimental import pallas as pl
from jax.experimental.pallas import tpu as pltpu
from jax.sharding import PartitionSpec as P

EPSILON = 1e-06
MIB = 1024 * 1024
NX, NZ, NH, NB = 4, 8, 4, 2
NE = NX * NZ
HEAD = 128
KEY_CHUNK = 256
LOG_ROWS = 16
MESH = pl.DeviceIdType.MESH
IN_VMEM = pl.BlockSpec(memory_space=pltpu.VMEM)
IN_ANY = pl.BlockSpec(memory_space=pl.ANY)
DMA = pltpu.SemaphoreType.DMA
NEAR_FIRST_Z = (1, 7, 2, 6, 3, 5, 4)
NEAR_FIRST_X = (1, 3, 2)


def remote(src, dst, send_sem, recv_sem, **where):
    return pltpu.make_async_remote_copy(
        src, dst, send_sem, recv_sem, device_id=where, device_id_type=MESH
    )


def here():
    expert = lax.axis_index("expert")
    return expert, expert // NX, lax.rem(expert, NX)


def signal(**where):
    pl.semaphore_signal(
        pltpu.get_barrier_semaphore(), inc=1, device_id=where, device_id_type=MESH
    )


def greet_experts(expert):
    @pl.loop(1, NE)
    def _(k):
        signal(expert=lax.rem(expert + k, NE))


def slot_matrix(routes, gates, experts, group):
    top, count = routes.shape
    names = lax.broadcasted_iota(jnp.int32, (experts, count), 0)
    chosen = jnp.zeros((experts, count), jnp.float32)
    gate = jnp.zeros((experts, count), jnp.float32)
    for k in range(top):
        hit = names == routes[k : k + 1, :]
        chosen = chosen + hit.astype(jnp.float32)
        gate = gate + jnp.where(hit, gates[k : k + 1, :], 0.0)
    earlier = lax.broadcasted_iota(jnp.int32, (count, count), 0)
    later = lax.broadcasted_iota(jnp.int32, (count, count), 1)
    before = ((earlier < later) & (earlier // group == later // group)).astype(jnp.bfloat16)
    rank = jnp.dot(chosen.astype(jnp.bfloat16), before, preferred_element_type=jnp.float32)
    place = chosen * (rank + 1.0)
    slots = 2 * (count // group)
    shape = (experts, slots, count)
    slot = lax.broadcasted_iota(jnp.int32, shape, 1)
    token = lax.broadcasted_iota(jnp.int32, shape, 2)
    wanted = (slot % 2 + 1).astype(jnp.float32)
    hits = (place[:, None, :] == wanted) & (token // group == slot // 2)
    places = hits.astype(jnp.float32)
    return places, places * gate[:, None, :]


def transposed_softmax(queries, keys, values_t, scores):
    count, rows = scores.shape
    chunks = range(0, count, KEY_CHUNK)
    top = jnp.full((8, rows), -jnp.inf, jnp.float32)
    for start in chunks:
        part = lax.dot_general(
            keys[start : start + KEY_CHUNK, :],
            queries,
            (((1,), (1,)), ((), ())),
            preferred_element_type=jnp.float32,
        )
        scores[start : start + KEY_CHUNK, :] = part
        top = jnp.maximum(top, jnp.max(part.reshape(KEY_CHUNK // 8, 8, rows), axis=0))
    peak = jnp.max(top, axis=0, keepdims=True)
    total = jnp.zeros((8, rows), jnp.float32)
    weighted = jnp.zeros((HEAD, rows), jnp.float32)
    for start in chunks:
        probs = jnp.exp(scores[start : start + KEY_CHUNK, :] - peak)
        total = total + jnp.sum(probs.reshape(KEY_CHUNK // 8, 8, rows), axis=0)
        weighted = weighted + jnp.dot(
            values_t[:, start : start + KEY_CHUNK],
            probs.astype(jnp.bfloat16),
            preferred_element_type=jnp.float32,
        )
    total = jnp.sum(total, axis=0, keepdims=True)
    return weighted / total, peak + jnp.log(total)


def with_log(average, log_total):
    rows = average.shape[1]
    high = log_total.astype(jnp.bfloat16).astype(jnp.float32)
    rest = log_total - high
    middle = rest.astype(jnp.bfloat16).astype(jnp.float32)
    low = rest - middle
    place = lax.broadcasted_iota(jnp.int32, (LOG_ROWS, rows), 0)
    tail = jnp.where(place == 0, high, jnp.where(place == 1, middle, low))
    return jnp.concatenate([average, tail], axis=0).astype(jnp.bfloat16)


def merged(blocks):
    logs = []
    for block in blocks:
        tail = block[HEAD : HEAD + LOG_ROWS].astype(jnp.float32)
        logs.append(tail[0:1] + tail[1:2] + tail[2:3])
    top = logs[0]
    for one in logs[1:]:
        top = jnp.maximum(top, one)
    shares = [jnp.exp(one - top) for one in logs]
    total = shares[0]
    for one in shares[1:]:
        total = total + one
    inverse = 1.0 / total
    result = None
    for block, share in zip(blocks, shares):
        term = block[:HEAD].astype(jnp.float32) * (share * inverse)
        result = term if result is None else result + term
    return result, top + jnp.log(total)


def layer_kernel(
    tokens, gain, w_query, q_gain, keys_h, values_h, output_h, post_gain, routes, gates,
    w_gate, w_up, w_down, out,
    scaled, weights, partial, arrived, queries, keys, values, values_t, output_weight, scores,
    average_s, average_x, merged_s, merged_z, attended, part, part_r, ordered, held_stream,
    places, mixing, gate_v, up_v, down_v, outgoing, stage, rows_all, normed, product, parts,
    back, returned, final_s, final_r,
    load, ts, tr, ws, wr, ps, pr, qs, qr, fqs, fqr,
    xas, xar, zas, zar, ms, mr, fms, fmr, hs, hr,
    es, er, fs, fr, gs, gr, bs, br, ys, yr,
):
    expert, z, x = here()
    head = lax.axis_index("head")
    core = lax.axis_index("batch")
    f32, bf16 = jnp.float32, jnp.bfloat16
    width = w_query.shape[1] // NX
    rows, features = tokens.shape
    block = queries.shape[2]
    span = rows // NZ
    heads_here = width // HEAD
    sub = span // NH
    count = NZ * sub
    others = [(i, j) for j in range(NB) for i in range(NH) if (i, j) != (0, 0)]

    def columns(owner):
        return pl.ds(pl.multiple_of(owner * width, width), width)

    own_weights = pltpu.make_async_copy(w_query.at[:, columns(x)], weights.at[x], load.at[0])
    own_weights.start()
    load_keys = pltpu.make_async_copy(keys_h, keys, load.at[1])
    load_values = pltpu.make_async_copy(values_h, values, load.at[2])
    load_output = pltpu.make_async_copy(output_h, output_weight, load.at[3])
    load_gate = pltpu.make_async_copy(w_gate, gate_v, load.at[4])
    load_up = pltpu.make_async_copy(w_up, up_v, load.at[5])
    load_down = pltpu.make_async_copy(w_down, down_v, load.at[6])

    @pl.loop(1, NE)
    def _(k):
        signal(expert=lax.rem(expert + k, NE))

    for i, j in others:
        signal(head=lax.rem(head + i, NH), batch=lax.rem(core + j, NB))
    scaled[x] = (tokens[...].astype(f32) * gain[...].astype(f32)).astype(bf16)
    pl.semaphore_wait(pltpu.get_barrier_semaphore(), NE - 1 + len(others))

    def weight_copy(owner, source):
        return remote(
            w_query.at[:, columns(owner)], weights.at[source], ws, wr, expert=z * NX + owner
        )

    def token_copy(target, source):
        return remote(scaled.at[source], scaled.at[source], ts, tr, expert=z * NX + target)

    def sum_copy(target, source):
        return remote(
            partial.at[target], arrived.at[source], ps, pr, expert=target * NX + x
        )

    def all_of(ref, send_sem, recv_sem):
        return remote(ref, ref, send_sem, recv_sem, expert=expert)

    for k in NEAR_FIRST_X:
        target = lax.rem(x + k, NX)
        token_copy(target, x).start()
        weight_copy(target, x).start()
    load_keys.start()
    load_values.start()
    load_output.start()
    slots = 2 * count // 8
    experts = NE * NB
    chosen, weighted = slot_matrix(routes[...], gates[...], experts, 8)
    places[...] = chosen.reshape(experts * slots, count).astype(bf16)
    flat = weighted.reshape(experts * slots, count)
    high = flat.astype(bf16)
    mixing[...] = jnp.concatenate([high, (flat - high.astype(f32)).astype(bf16)], axis=1)
    own_weights.wait()
    all_of(scaled.at[pl.ds(0, NX - 1)], ts, tr).wait_recv()
    all_of(weights.at[pl.ds(0, NX - 1)], ws, wr).wait_recv()
    left = jnp.concatenate([scaled[i] for i in range(NX)], axis=1)
    right = weights[...].reshape(NX * features, width)
    partial[...] = jnp.dot(left, right, preferred_element_type=f32).reshape(NZ, span, width)
    for k in NEAR_FIRST_Z:
        sum_copy(lax.rem(z + k, NZ), z).start()
    arrived[z] = partial[z]
    load_gate.start()
    load_up.start()
    load_down.start()
    load_values.wait()
    for i in range(0, values.shape[0], 128):
        values_t[:, i : i + 128] = values[i : i + 128, :].astype(f32).T.astype(bf16)
    all_of(scaled.at[pl.ds(0, NX - 1)], ts, tr).wait_send()
    all_of(weights.at[pl.ds(0, NX - 1)], ws, wr).wait_send()
    load_keys.wait()
    load_output.wait()
    all_of(arrived.at[pl.ds(0, NZ - 1)], ps, pr).wait_recv()
    total = arrived[0]
    for i in range(1, NZ):
        total = total + arrived[i]
    factor = q_gain[...].astype(f32) / jnp.sqrt(f32(HEAD))
    heads = []
    for h in range(heads_here):
        one = total[:, h * HEAD : (h + 1) * HEAD]
        mean = jnp.mean(one * one, axis=-1, keepdims=True)
        heads.append(one * lax.rsqrt(mean + EPSILON) * factor)
    queries[x, z] = jnp.concatenate(heads, axis=0).astype(bf16)

    def at_step(n):
        near = (n + 1) // 2
        return lax.rem(z + jnp.where(n % 2 == 1, near, NZ - near), NZ)

    def spread(blocks, send_sem, recv_sem):
        for k in NEAR_FIRST_Z:
            remote(
                blocks.at[x, z], blocks.at[x, z], send_sem, recv_sem.at[z],
                expert=lax.rem(z + k, NZ) * NX + x,
            ).start()

    def pass_on(blocks, z_sems, send_sem, recv_sem, n):
        r = at_step(n)
        block = blocks.at[x, r]

        @pl.when(n >= 1)
        def _():
            all_of(block, z_sems[0], z_sems[1].at[r]).wait_recv()

        for k in NEAR_FIRST_X:
            remote(
                block, block, send_sem, recv_sem.at[r], expert=z * NX + lax.rem(x + k, NX)
            ).start()

    def passed(blocks, send_sem, recv_sem, n):
        r = at_step(n)
        return all_of(blocks.at[pl.ds(0, NX - 1), r], send_sem, recv_sem.at[r])

    def attend(n):
        r = at_step(n)
        here_rows = queries[:, r].reshape(NX * block, HEAD)
        average, log_total = transposed_softmax(here_rows, keys, values_t, scores)
        both = with_log(average, log_total)
        for i in range(NX):
            average_s[r, i] = both[:, i * block : (i + 1) * block]
        for k in NEAR_FIRST_X:
            target = lax.rem(x + k, NX)
            remote(
                average_s.at[r, target], average_x.at[r, x], xas, xar.at[r],
                expert=z * NX + target,
            ).start()
        average_x[r, x] = average_s[r, x]

    def merge_x(n):
        r = at_step(n)
        all_of(average_x.at[r, pl.ds(0, NX - 1)], xas, xar.at[r]).wait_recv()
        average, log_total = merged([average_x[r, i] for i in range(NX)])
        merged_s[r] = with_log(average, log_total)

        @pl.when(n == 0)
        def _():
            merged_z[z] = merged_s[z]

        @pl.when(n >= 1)
        def _():
            remote(merged_s.at[r], merged_z.at[z], zas, zar, expert=r * NX + x).start()

    parts_of_z = 2
    per_part = NZ // parts_of_z

    def project(which):
        tall = []
        for n in range(which * per_part, (which + 1) * per_part):
            passed(attended, fms, fmr, n).wait_recv()
            r = at_step(n)
            tall.append(
                jnp.concatenate(
                    [
                        attended[i, r, j * span : (j + 1) * span, :]
                        for i in range(NX)
                        for j in range(heads_here)
                    ],
                    axis=1,
                )
            )
        left = jnp.concatenate(tall, axis=0)
        made = jnp.dot(left, output_weight[...], preferred_element_type=f32)
        made = made.reshape(per_part, NH, sub, features)
        for i in range(NH):
            part[which, i] = made[:, i].reshape(per_part * sub, features)
        for k in (1, 3, 2):
            target = lax.rem(head + k, NH)
            remote(
                part.at[which, target], part_r.at[which, head], hs, hr.at[which], head=target
            ).start()
        part_r[which, head] = part[which, head]

    groups = er.shape[0]
    per_group = NE // groups
    own_group = expert // per_group
    me_hb = head * NB + core
    most = len(others)

    def group_of(step):
        return lax.rem(own_group + step, groups)

    def members(g):
        return pl.ds(g * per_group, per_group)

    def half(owner):
        return pl.ds(pl.multiple_of(owner * slots, slots), slots)

    def target_of(i, j):
        return lax.rem(head + i, NH), lax.rem(core + j, NB)

    def dispatch():
        for which in range(parts_of_z):
            all_of(part_r.at[which, pl.ds(0, NH - 1)], hs, hr.at[which]).wait_recv()
            summed = part_r[which, 0]
            for i in range(1, NH):
                summed = summed + part_r[which, i]
            summed = summed.reshape(per_part, sub, features)
            for n in range(per_part):
                ordered[at_step(which * per_part + n)] = summed[n]
        resid = tokens[...].astype(f32).reshape(NZ, NH, sub, features)
        mine = jnp.zeros((NZ, sub, features), f32)
        for i in range(NH):
            mine = jnp.where(head == i, resid[:, i], mine)
        held_stream[...] = (mine + ordered[...]).reshape(count, features).astype(bf16)
        picked = jnp.dot(places[...], held_stream[...], preferred_element_type=f32)
        outgoing[...] = picked.astype(bf16).reshape(NE, NB * slots, features)

        @pl.loop(1, NE)
        def _(k):
            target = lax.rem(expert + k, NE)
            remote(
                outgoing.at[target], stage.at[expert], es, er.at[own_group], expert=target
            ).start()

        stage[expert] = outgoing[expert]

    def forward():
        @pl.loop(0, groups)
        def _(step):
            g = group_of(step)

            @pl.when(step == 0)
            def _():
                few = stage.at[pl.ds(0, per_group - 1)]
                all_of(few, es, er.at[g]).wait_recv()

            @pl.when(step != 0)
            def _():
                all_of(stage.at[members(g)], es, er.at[g]).wait_recv()

            for i, j in others:
                to_head, to_core = target_of(i, j)
                remote(
                    stage.at[members(g), half(to_core)],
                    rows_all.at[me_hb, members(g)],
                    fs,
                    fr.at[g],
                    head=to_head,
                    batch=to_core,
                ).start()
            rows_all[me_hb, members(g)] = stage[members(g), half(core)]

    ahead = 2
    spread(queries, qs, qr)
    for n in range(ahead):
        pass_on(queries, (qs, qr), fqs, fqr, n)

    @pl.loop(0, NZ)
    def _(n):
        @pl.when(n + ahead < NZ)
        def _():
            pass_on(queries, (qs, qr), fqs, fqr, n + ahead)

        passed(queries, fqs, fqr, n).wait_recv()
        attend(n)

        @pl.when(n >= 1)
        def _():
            merge_x(n - 1)

    merge_x(NZ - 1)
    all_of(queries.at[0, pl.ds(0, NZ - 1)], qs, qr.at[0]).wait_send()
    all_of(queries.at[pl.ds(0, NX - 1)], fqs, fqr.at[0]).wait_send()
    all_of(average_s.at[:, pl.ds(0, NX - 1)], xas, xar.at[0]).wait_send()
    all_of(arrived.at[pl.ds(0, NZ - 1)], ps, pr).wait_send()
    all_of(merged_z.at[pl.ds(0, NZ - 1)], zas, zar).wait_recv()
    average, _ = merged([merged_z[i] for i in range(NZ)])
    attended[x, z] = average.T.astype(bf16)
    spread(attended, ms, mr)
    for n in range(NZ):
        pass_on(attended, (ms, mr), fms, fmr, n)
    for which in range(parts_of_z):
        project(which)
    dispatch()
    load_gate.wait()
    load_up.wait()
    load_down.wait()
    all_of(merged_s.at[pl.ds(0, NZ - 1)], zas, zar).wait_send()
    all_of(attended.at[0, pl.ds(0, NZ - 1)], ms, mr.at[0]).wait_send()
    all_of(attended.at[pl.ds(0, NX - 1)], fms, fmr.at[0]).wait_send()
    all_of(part.at[:, pl.ds(0, NH - 1)], hs, hr.at[0]).wait_send()
    forward()
    all_of(outgoing.at[pl.ds(0, NE - 1)], es, er.at[0]).wait_send()

    held = NH * NB * slots
    square = jnp.zeros((held, features), f32)
    for g in range(groups):
        for e in range(g * per_group, (g + 1) * per_group):
            if e == g * per_group:
                all_of(rows_all.at[pl.ds(0, most), members(g)], fs, fr.at[g]).wait_recv()
            wide = rows_all[:, e].reshape(held, features).astype(f32)
            square = square + wide * wide
    mean = jnp.sum(square, axis=1, keepdims=True) * (1.0 / (NE * features))
    scale = lax.rsqrt(mean + EPSILON)
    for e in range(NE):
        wide = rows_all[:, e].reshape(held, features).astype(f32)
        normed[:, e * features : (e + 1) * features] = (
            wide * scale * post_gain[e : e + 1, :].astype(f32)
        ).astype(bf16)
    gate_part = jnp.dot(normed[...], gate_v[...], preferred_element_type=f32)
    up_part = jnp.dot(normed[...], up_v[...], preferred_element_type=f32)
    hidden = (gate_part / (1.0 + jnp.exp(-gate_part)) * up_part).astype(bf16)
    reach = parts.shape[-1]
    bands = parts.shape[0]
    per_band = NE // bands

    for g in range(bands):
        made = jnp.dot(hidden, down_v[:, g * reach : (g + 1) * reach], preferred_element_type=f32)
        product[g] = made.astype(bf16).reshape(NH * NB, slots, reach)
        for i, j in others:
            to_head, to_core = target_of(i, j)
            remote(
                product.at[g, to_head * NB + to_core],
                parts.at[g, me_hb],
                gs,
                gr.at[g],
                head=to_head,
                batch=to_core,
            ).start()
        parts[g, me_hb] = product[g, me_hb]

    for g in range(bands):
        all_of(parts.at[g, pl.ds(0, most)], gs, gr.at[g]).wait_recv()
        total = parts[g, 0:NB].astype(f32)
        for i in range(1, NH):
            total = total + parts[g, i * NB : (i + 1) * NB].astype(f32)
        total = total.reshape(NB * slots, reach).astype(bf16)
        for k in range(per_band):
            back[g * per_band + k] = total[:, k * features : (k + 1) * features]

        @pl.loop(0, per_band)
        def _(k):
            target = g * per_band + k

            @pl.when(target != expert)
            def _():
                remote(back.at[target], returned.at[expert], bs, br, expert=target).start()

    returned[expert] = back[expert]
    all_of(rows_all.at[pl.ds(0, most)], fs, fr.at[0]).wait_send()
    all_of(product.at[:, pl.ds(0, most)], gs, gr.at[0]).wait_send()
    all_of(returned.at[pl.ds(0, NE - 1)], bs, br).wait_recv()
    both = lax.dot_general(
        mixing[...],
        returned[...].reshape(experts * slots, features),
        (((0,), (0,)), ((), ())),
        preferred_element_type=f32,
    )
    mixture = both[:count] + both[count:]
    final_s[...] = (held_stream[...].astype(f32) + mixture).astype(bf16)
    for k in (1, 3, 2):
        remote(final_s, final_r.at[head], ys, yr, head=lax.rem(head + k, NH)).start()
    final_r[head] = final_s[...]
    all_of(back.at[pl.ds(0, NE - 1)], bs, br).wait_send()
    all_of(final_r.at[pl.ds(0, NH - 1)], ys, yr).wait_recv()
    pieces = [final_r[i].astype(f32).reshape(NZ, sub, features) for i in range(NH)]
    out[...] = jnp.concatenate(
        [pieces[i][r] for r in range(NZ) for i in range(NH)], axis=0
    ).astype(bf16)
    all_of(final_r.at[pl.ds(0, NH - 1)], ys, yr).wait_send()


def on_device(
    tokens, attn_gain, w_query, q_gain, cached_keys, prefix_values, output_weight,
    post_gain, routes, route_gates, w_gate, w_up, w_down,
):
    rows, features = tokens.shape
    width = w_query.shape[1] // NX
    block = rows * w_query.shape[1] // HEAD // NE
    bf16, f32 = jnp.bfloat16, jnp.float32
    keys = cached_keys.shape[0]
    span = rows // NZ
    sub = span // NH
    count = NZ * sub
    halves = 2
    head = lax.axis_index("head")
    top = routes.shape[1]

    def mine(table):
        cut = lax.dynamic_index_in_dim(table.reshape(NZ, NH, sub, top), head, 1, False)
        return cut.reshape(count, top).T

    model, ff = w_gate.shape[1:]
    slots = 2 * count // 8
    groups = 2
    bands = 4
    experts = NE * NB
    V = pltpu.VMEM
    return pl.pallas_call(
        layer_kernel,
        out_shape=jax.ShapeDtypeStruct((rows, features), bf16),
        in_specs=[IN_VMEM, IN_VMEM, IN_ANY, IN_VMEM] + [IN_ANY] * 3 + [IN_VMEM] * 3 + [IN_ANY] * 3,
        out_specs=IN_VMEM,
        scratch_shapes=[
            V((NX, rows, features), bf16),
            V((NX, features, width), bf16),
            V((NZ, span, width), f32),
            V((NZ, span, width), f32),
            V((NX, NZ, block, HEAD), bf16),
            V((keys, HEAD), bf16),
            V((keys, HEAD), bf16),
            V((HEAD, keys), bf16),
            V(output_weight.shape, bf16),
            V((keys, NX * block), f32),
            V((NZ, NX, HEAD + LOG_ROWS, block), bf16),
            V((NZ, NX, HEAD + LOG_ROWS, block), bf16),
            V((NZ, HEAD + LOG_ROWS, block), bf16),
            V((NZ, HEAD + LOG_ROWS, block), bf16),
            V((NX, NZ, block, HEAD), bf16),
            V((halves, NH, count // halves, features), f32),
            V((halves, NH, count // halves, features), f32),
            V((NZ, sub, features), f32),
            V((count, features), bf16),
            V((experts * slots, count), bf16),
            V((experts * slots, 2 * count), bf16),
            V((model, ff), bf16),
            V((model, ff), bf16),
            V((ff, model), bf16),
            V((NE, NB * slots, features), bf16),
            V((NE, NB * slots, features), bf16),
            V((NH * NB, NE, slots, features), bf16),
            V((NH * NB * slots, model), bf16),
            V((bands, NH * NB, slots, model // bands), bf16),
            V((bands, NH * NB, slots, model // bands), bf16),
            V((NE, NB * slots, features), bf16),
            V((NE, NB * slots, features), bf16),
            V((count, features), bf16),
            V((NH, count, features), bf16),
            DMA((7,)),
            DMA, DMA, DMA, DMA,
            DMA, DMA,
            DMA, DMA((NZ,)), DMA, DMA((NZ,)),
            DMA, DMA((NZ,)), DMA, DMA,
            DMA, DMA((NZ,)), DMA, DMA((NZ,)),
            DMA, DMA((halves,)),
            DMA, DMA((groups,)), DMA, DMA((groups,)),
            DMA, DMA((bands,)), DMA, DMA, DMA, DMA,
        ],
        compiler_params=pltpu.CompilerParams(
            collective_id=1, has_side_effects=True, vmem_limit_bytes=56 * MIB
        ),
        name="scoring_layer",
    )(
        tokens, attn_gain[None, :], w_query, q_gain[None, :],
        cached_keys, prefix_values, output_weight,
        post_gain.reshape(NE, features), mine(routes), mine(route_gates),
        w_gate[0], w_up[0], w_down[0],
    )


def solution(mesh):
    placed = (
        P("batch", "expert"),
        P("expert"),
        P("expert", "head"),
        P(),
        P("expert", "head"),
        P("expert", "head"),
        P("head", "expert"),
        P(),
        P("batch", None),
        P("batch", None),
        P(("expert", "batch"), None, "head"),
        P(("expert", "batch"), None, "head"),
        P(("expert", "batch"), "head", None),
    )
    return jax.shard_map(
        on_device, mesh=mesh, in_specs=placed, out_specs=P("batch", "expert"), check_vma=False
    )
```

```python
import functools

import jax
import jax.numpy as jnp
from jax import lax
from jax.experimental import pallas as pl
from jax.experimental.pallas import tpu as pltpu
from jax.sharding import PartitionSpec as P

EPSILON = 1e-06
MIB = 1024 * 1024
NX, NZ, NH, NB = 4, 8, 4, 2
NE = NX * NZ
HEAD = 128
KEY_CHUNK = 256
LOG_ROWS = 16
MESH = pl.DeviceIdType.MESH
IN_VMEM = pl.BlockSpec(memory_space=pltpu.VMEM)
IN_ANY = pl.BlockSpec(memory_space=pl.ANY)
DMA = pltpu.SemaphoreType.DMA
NEAR_FIRST_Z = (1, 7, 2, 6, 3, 5, 4)
NEAR_FIRST_X = (1, 3, 2)
ATTEND_ORDER = (0, 1, 6, 4, 3, 5, 2, 7)


def remote(src, dst, send_sem, recv_sem, **where):
    return pltpu.make_async_remote_copy(
        src, dst, send_sem, recv_sem, device_id=where, device_id_type=MESH
    )


def here():
    expert = lax.axis_index("expert")
    return expert, expert // NX, lax.rem(expert, NX)


def signal(**where):
    pl.semaphore_signal(
        pltpu.get_barrier_semaphore(), inc=1, device_id=where, device_id_type=MESH
    )


def greet_experts(expert):
    @pl.loop(1, NE)
    def _(k):
        signal(expert=lax.rem(expert + k, NE))


def slot_matrix(routes, gates, experts, group):
    top, count = routes.shape
    names = lax.broadcasted_iota(jnp.int32, (experts, count), 0)
    chosen = jnp.zeros((experts, count), jnp.float32)
    gate = jnp.zeros((experts, count), jnp.float32)
    for k in range(top):
        hit = names == routes[k : k + 1, :]
        chosen = chosen + hit.astype(jnp.float32)
        gate = gate + jnp.where(hit, gates[k : k + 1, :], 0.0)
    earlier = lax.broadcasted_iota(jnp.int32, (count, count), 0)
    later = lax.broadcasted_iota(jnp.int32, (count, count), 1)
    before = ((earlier < later) & (earlier // group == later // group)).astype(jnp.bfloat16)
    rank = jnp.dot(chosen.astype(jnp.bfloat16), before, preferred_element_type=jnp.float32)
    place = chosen * (rank + 1.0)
    slots = 2 * (count // group)
    shape = (experts, slots, count)
    slot = lax.broadcasted_iota(jnp.int32, shape, 1)
    token = lax.broadcasted_iota(jnp.int32, shape, 2)
    wanted = (slot % 2 + 1).astype(jnp.float32)
    hits = (place[:, None, :] == wanted) & (token // group == slot // 2)
    places = hits.astype(jnp.float32)
    return places, places * gate[:, None, :]


def transposed_softmax(queries, keys, values_t, scores):
    count, rows = scores.shape
    chunks = range(0, count, KEY_CHUNK)
    top = jnp.full((8, rows), -jnp.inf, jnp.float32)
    for start in chunks:
        part = lax.dot_general(
            keys[start : start + KEY_CHUNK, :],
            queries,
            (((1,), (1,)), ((), ())),
            preferred_element_type=jnp.float32,
        )
        scores[start : start + KEY_CHUNK, :] = part
        top = jnp.maximum(top, jnp.max(part.reshape(KEY_CHUNK // 8, 8, rows), axis=0))
    peak = jnp.max(top, axis=0, keepdims=True)
    total = jnp.zeros((8, rows), jnp.float32)
    weighted = jnp.zeros((HEAD, rows), jnp.float32)
    for start in chunks:
        probs = jnp.exp(scores[start : start + KEY_CHUNK, :] - peak)
        total = total + jnp.sum(probs.reshape(KEY_CHUNK // 8, 8, rows), axis=0)
        weighted = weighted + jnp.dot(
            values_t[:, start : start + KEY_CHUNK],
            probs.astype(jnp.bfloat16),
            preferred_element_type=jnp.float32,
        )
    total = jnp.sum(total, axis=0, keepdims=True)
    return weighted / total, peak + jnp.log(total)


def with_log(average, log_total):
    rows = average.shape[1]
    high = log_total.astype(jnp.bfloat16).astype(jnp.float32)
    rest = log_total - high
    middle = rest.astype(jnp.bfloat16).astype(jnp.float32)
    low = rest - middle
    place = lax.broadcasted_iota(jnp.int32, (LOG_ROWS, rows), 0)
    tail = jnp.where(place == 0, high, jnp.where(place == 1, middle, low))
    return jnp.concatenate([average, tail], axis=0).astype(jnp.bfloat16)


def merged(blocks):
    logs = []
    for block in blocks:
        tail = block[HEAD : HEAD + LOG_ROWS].astype(jnp.float32)
        logs.append(tail[0:1] + tail[1:2] + tail[2:3])
    top = logs[0]
    for one in logs[1:]:
        top = jnp.maximum(top, one)
    shares = [jnp.exp(one - top) for one in logs]
    total = shares[0]
    for one in shares[1:]:
        total = total + one
    inverse = 1.0 / total
    result = None
    for block, share in zip(blocks, shares):
        term = block[:HEAD].astype(jnp.float32) * (share * inverse)
        result = term if result is None else result + term
    return result, top + jnp.log(total)


def layer_kernel(
    tokens, gain, w_query, q_gain, keys_h, values_h, output_h, post_gain, routes, gates,
    w_gate, w_up, w_down, out,
    scaled, weights, partial, arrived, queries, keys, values, values_t, output_weight, scores,
    average_s, average_x, merged_s, merged_z, attended, part, part_r, ordered, held_stream,
    places, mixing, gate_v, up_v, down_v, outgoing, stage, rows_all, normed, product, parts,
    back, returned, final_s, final_r,
    load, ts, tr, ws, wr, ps, pr, qs, qr, fqs, fqr,
    xas, xar, zas, zar, ms, mr, fms, fmr, hs, hr,
    es, er, fs, fr, gs, gr, bs, br, ys, yr,
):
    expert, z, x = here()
    head = lax.axis_index("head")
    core = lax.axis_index("batch")
    f32, bf16 = jnp.float32, jnp.bfloat16
    width = w_query.shape[1] // NX
    rows, features = tokens.shape
    block = queries.shape[2]
    span = rows // NZ
    heads_here = width // HEAD
    sub = span // NH
    count = NZ * sub
    others = [(i, j) for j in range(NB) for i in range(NH) if (i, j) != (0, 0)]

    def columns(owner):
        return pl.ds(pl.multiple_of(owner * width, width), width)

    own_weights = pltpu.make_async_copy(w_query.at[:, columns(x)], weights.at[x], load.at[0])
    own_weights.start()
    load_keys = pltpu.make_async_copy(keys_h, keys, load.at[1])
    load_values = pltpu.make_async_copy(values_h, values, load.at[2])
    load_output = pltpu.make_async_copy(output_h, output_weight, load.at[3])
    load_gate = pltpu.make_async_copy(w_gate, gate_v, load.at[4])
    load_up = pltpu.make_async_copy(w_up, up_v, load.at[5])
    load_down = pltpu.make_async_copy(w_down, down_v, load.at[6])

    @pl.loop(1, NE)
    def _(k):
        signal(expert=lax.rem(expert + k, NE))

    for i, j in others:
        signal(head=lax.rem(head + i, NH), batch=lax.rem(core + j, NB))
    scaled[x] = (tokens[...].astype(f32) * gain[...].astype(f32)).astype(bf16)
    pl.semaphore_wait(pltpu.get_barrier_semaphore(), NE - 1 + len(others))

    def weight_copy(owner, source):
        return remote(
            w_query.at[:, columns(owner)], weights.at[source], ws, wr, expert=z * NX + owner
        )

    def token_copy(target, source):
        return remote(scaled.at[source], scaled.at[source], ts, tr, expert=z * NX + target)

    def sum_copy(target, source):
        return remote(
            partial.at[target], arrived.at[source], ps, pr, expert=target * NX + x
        )

    def all_of(ref, send_sem, recv_sem):
        return remote(ref, ref, send_sem, recv_sem, expert=expert)

    for k in NEAR_FIRST_X:
        target = lax.rem(x + k, NX)
        token_copy(target, x).start()
        weight_copy(target, x).start()
    load_keys.start()
    load_values.start()
    load_output.start()
    own_weights.wait()
    all_of(scaled.at[pl.ds(0, NX - 1)], ts, tr).wait_recv()
    all_of(weights.at[pl.ds(0, NX - 1)], ws, wr).wait_recv()
    left = jnp.concatenate([scaled[i] for i in range(NX)], axis=1)
    right = weights[...].reshape(NX * features, width)
    partial[...] = jnp.dot(left, right, preferred_element_type=f32).reshape(NZ, span, width)
    for k in NEAR_FIRST_Z:
        sum_copy(lax.rem(z + k, NZ), z).start()
    arrived[z] = partial[z]
    load_gate.start()
    load_up.start()
    load_down.start()
    slots = 2 * count // 8
    experts = NE * NB
    token = lax.broadcasted_iota(jnp.int32, (rows, count), 0)
    owned = lax.broadcasted_iota(jnp.int32, (rows, count), 1)
    mine = (token == owned // sub * span + head * sub + owned % sub).astype(f32)

    def own(table):
        return jnp.dot(
            table, mine, precision=lax.Precision.HIGHEST, preferred_element_type=f32
        )

    own_routes = own(routes[...].astype(f32)).astype(jnp.int32)
    chosen, weighted = slot_matrix(own_routes, own(gates[...]), experts, 8)
    places[...] = chosen.reshape(experts * slots, count).astype(bf16)
    flat = weighted.reshape(experts * slots, count)
    high = flat.astype(bf16)
    mixing[...] = jnp.concatenate([high, (flat - high.astype(f32)).astype(bf16)], axis=1)
    load_values.wait()
    for i in range(0, values.shape[0], 128):
        values_t[:, i : i + 128] = values[i : i + 128, :].astype(f32).T.astype(bf16)
    all_of(scaled.at[pl.ds(0, NX - 1)], ts, tr).wait_send()
    all_of(weights.at[pl.ds(0, NX - 1)], ws, wr).wait_send()
    load_keys.wait()
    load_output.wait()
    all_of(arrived.at[pl.ds(0, NZ - 1)], ps, pr).wait_recv()
    total = arrived[0]
    for i in range(1, NZ):
        total = total + arrived[i]
    factor = q_gain[...].astype(f32) / jnp.sqrt(f32(HEAD))
    heads = []
    for h in range(heads_here):
        one = total[:, h * HEAD : (h + 1) * HEAD]
        mean = jnp.mean(one * one, axis=-1, keepdims=True)
        heads.append(one * lax.rsqrt(mean + EPSILON) * factor)
    queries[x, z] = jnp.concatenate(heads, axis=0).astype(bf16)

    def at_step(n):
        near = (n + 1) // 2
        return lax.rem(z + jnp.where(n % 2 == 1, near, NZ - near), NZ)

    def at_turn(n):
        offset = ATTEND_ORDER[NZ - 1]
        for i in range(NZ - 1):
            offset = jnp.where(n == i, ATTEND_ORDER[i], offset)
        return lax.rem(z + offset, NZ)

    def spread(blocks, send_sem, recv_sem):
        for k in NEAR_FIRST_Z:
            remote(
                blocks.at[x, z], blocks.at[x, z], send_sem, recv_sem.at[z],
                expert=lax.rem(z + k, NZ) * NX + x,
            ).start()

    def pass_on(blocks, z_sems, send_sem, recv_sem, n, order):
        r = order(n)
        block = blocks.at[x, r]

        @pl.when(n >= 1)
        def _():
            all_of(block, z_sems[0], z_sems[1].at[r]).wait_recv()

        for k in NEAR_FIRST_X:
            remote(
                block, block, send_sem, recv_sem.at[r], expert=z * NX + lax.rem(x + k, NX)
            ).start()

    def passed(blocks, send_sem, recv_sem, n, order):
        r = order(n)
        return all_of(blocks.at[pl.ds(0, NX - 1), r], send_sem, recv_sem.at[r])

    def attend(n):
        r = at_turn(n)
        here_rows = queries[:, r].reshape(NX * block, HEAD)
        average, log_total = transposed_softmax(here_rows, keys, values_t, scores)
        both = with_log(average, log_total)
        for i in range(NX):
            average_s[r, i] = both[:, i * block : (i + 1) * block]
        for k in NEAR_FIRST_X:
            target = lax.rem(x + k, NX)
            remote(
                average_s.at[r, target], average_x.at[r, x], xas, xar.at[r],
                expert=z * NX + target,
            ).start()
        average_x[r, x] = average_s[r, x]

    def merge_x(n):
        r = at_turn(n)
        all_of(average_x.at[r, pl.ds(0, NX - 1)], xas, xar.at[r]).wait_recv()
        average, log_total = merged([average_x[r, i] for i in range(NX)])
        merged_s[r] = with_log(average, log_total)

        @pl.when(n == 0)
        def _():
            merged_z[z] = merged_s[z]

        @pl.when(n >= 1)
        def _():
            remote(merged_s.at[r], merged_z.at[z], zas, zar, expert=r * NX + x).start()

    parts_of_z = 2
    per_part = NZ // parts_of_z

    def project(which):
        tall = []
        for n in range(which * per_part, (which + 1) * per_part):
            passed(attended, fms, fmr, n, at_step).wait_recv()
            r = at_step(n)
            tall.append(
                jnp.concatenate(
                    [
                        attended[i, r, j * span : (j + 1) * span, :]
                        for i in range(NX)
                        for j in range(heads_here)
                    ],
                    axis=1,
                )
            )
        left = jnp.concatenate(tall, axis=0)
        made = jnp.dot(left, output_weight[...], preferred_element_type=f32)
        made = made.reshape(per_part, NH, sub, features)
        for i in range(NH):
            part[which, i] = made[:, i].reshape(per_part * sub, features)
        for k in (1, 3, 2):
            target = lax.rem(head + k, NH)
            remote(
                part.at[which, target], part_r.at[which, head], hs, hr.at[which], head=target
            ).start()
        part_r[which, head] = part[which, head]

    groups = er.shape[0]
    per_group = NE // groups
    own_group = expert // per_group
    me_hb = head * NB + core
    most = len(others)

    def group_of(step):
        return lax.rem(own_group + step, groups)

    def members(g):
        return pl.ds(g * per_group, per_group)

    def half(owner):
        return pl.ds(pl.multiple_of(owner * slots, slots), slots)

    def target_of(i, j):
        return lax.rem(head + i, NH), lax.rem(core + j, NB)

    def dispatch():
        for which in range(parts_of_z):
            all_of(part_r.at[which, pl.ds(0, NH - 1)], hs, hr.at[which]).wait_recv()
            summed = part_r[which, 0]
            for i in range(1, NH):
                summed = summed + part_r[which, i]
            summed = summed.reshape(per_part, sub, features)
            for n in range(per_part):
                ordered[at_step(which * per_part + n)] = summed[n]
        resid = tokens[...].astype(f32).reshape(NZ, NH, sub, features)
        mine = jnp.zeros((NZ, sub, features), f32)
        for i in range(NH):
            mine = jnp.where(head == i, resid[:, i], mine)
        held_stream[...] = (mine + ordered[...]).reshape(count, features).astype(bf16)
        picked = jnp.dot(places[...], held_stream[...], preferred_element_type=f32)
        outgoing[...] = picked.astype(bf16).reshape(NE, NB * slots, features)

        @pl.loop(0, NE - 1)
        def _(n):
            step = (n + 1) // 2
            k = NE // 2 + jnp.where(n % 2 == 1, step, -step)
            target = lax.rem(expert + k, NE)
            remote(
                outgoing.at[target], stage.at[expert], es, er.at[own_group], expert=target
            ).start()

        stage[expert] = outgoing[expert]

    def forward():
        @pl.loop(0, groups)
        def _(step):
            g = group_of(step)

            @pl.when(step == 0)
            def _():
                few = stage.at[pl.ds(0, per_group - 1)]
                all_of(few, es, er.at[g]).wait_recv()

            @pl.when(step != 0)
            def _():
                all_of(stage.at[members(g)], es, er.at[g]).wait_recv()

            for i, j in others:
                to_head, to_core = target_of(i, j)
                remote(
                    stage.at[members(g), half(to_core)],
                    rows_all.at[me_hb, members(g)],
                    fs,
                    fr.at[g],
                    head=to_head,
                    batch=to_core,
                ).start()
            rows_all[me_hb, members(g)] = stage[members(g), half(core)]

    ahead = 2
    spread(queries, qs, qr)
    for n in range(ahead):
        pass_on(queries, (qs, qr), fqs, fqr, n, at_turn)

    @pl.loop(0, NZ)
    def _(n):
        @pl.when(n + ahead < NZ)
        def _():
            pass_on(queries, (qs, qr), fqs, fqr, n + ahead, at_turn)

        passed(queries, fqs, fqr, n, at_turn).wait_recv()
        attend(n)

        @pl.when(n >= 2)
        def _():
            merge_x(n - 2)

    merge_x(NZ - 2)
    merge_x(NZ - 1)
    all_of(queries.at[0, pl.ds(0, NZ - 1)], qs, qr.at[0]).wait_send()
    all_of(queries.at[pl.ds(0, NX - 1)], fqs, fqr.at[0]).wait_send()
    all_of(average_s.at[:, pl.ds(0, NX - 1)], xas, xar.at[0]).wait_send()
    all_of(arrived.at[pl.ds(0, NZ - 1)], ps, pr).wait_send()
    all_of(merged_z.at[pl.ds(0, NZ - 1)], zas, zar).wait_recv()
    average, _ = merged([merged_z[i] for i in range(NZ)])
    attended[x, z] = average.T.astype(bf16)
    spread(attended, ms, mr)
    for n in range(NZ):
        pass_on(attended, (ms, mr), fms, fmr, n, at_step)
    for which in range(parts_of_z):
        project(which)
    dispatch()
    load_gate.wait()
    load_up.wait()
    load_down.wait()
    all_of(merged_s.at[pl.ds(0, NZ - 1)], zas, zar).wait_send()
    all_of(attended.at[0, pl.ds(0, NZ - 1)], ms, mr.at[0]).wait_send()
    all_of(attended.at[pl.ds(0, NX - 1)], fms, fmr.at[0]).wait_send()
    all_of(part.at[:, pl.ds(0, NH - 1)], hs, hr.at[0]).wait_send()
    forward()
    all_of(outgoing.at[pl.ds(0, NE - 1)], es, er.at[0]).wait_send()

    held = NH * NB * slots
    square = jnp.zeros((held, features), f32)
    for g in range(groups):
        for e in range(g * per_group, (g + 1) * per_group):
            if e == g * per_group:
                all_of(rows_all.at[pl.ds(0, most), members(g)], fs, fr.at[g]).wait_recv()
            wide = rows_all[:, e].reshape(held, features).astype(f32)
            square = square + wide * wide
    mean = jnp.sum(square, axis=1, keepdims=True) * (1.0 / (NE * features))
    scale = lax.rsqrt(mean + EPSILON)
    for e in range(NE):
        wide = rows_all[:, e].reshape(held, features).astype(f32)
        normed[:, e * features : (e + 1) * features] = (
            wide * scale * post_gain[e : e + 1, :].astype(f32)
        ).astype(bf16)
    gate_part = jnp.dot(normed[...], gate_v[...], preferred_element_type=f32)
    up_part = jnp.dot(normed[...], up_v[...], preferred_element_type=f32)
    hidden = (gate_part / (1.0 + jnp.exp(-gate_part)) * up_part).astype(bf16)
    reach = parts.shape[-1]
    bands = parts.shape[0]
    per_band = NE // bands

    own_band = expert // per_band
    band_order = [lax.rem(own_band + i, bands) for i in (2, 1, 3, 0)]
    for g in band_order:
        lanes = pl.ds(pl.multiple_of(g * reach, reach), reach)
        made = jnp.dot(hidden, down_v[:, lanes], preferred_element_type=f32)
        product[g] = made.astype(bf16).reshape(NH * NB, slots, reach)
        for i, j in others:
            to_head, to_core = target_of(i, j)
            remote(
                product.at[g, to_head * NB + to_core],
                parts.at[g, me_hb],
                gs,
                gr.at[g],
                head=to_head,
                batch=to_core,
            ).start()
        parts[g, me_hb] = product[g, me_hb]

    for g in band_order:
        all_of(parts.at[g, pl.ds(0, most)], gs, gr.at[g]).wait_recv()
        total = parts[g, pl.ds(0, NB)].astype(f32)
        for i in range(1, NH):
            total = total + parts[g, pl.ds(i * NB, NB)].astype(f32)
        total = total.reshape(NB * slots, reach).astype(bf16)
        for k in range(per_band):
            back[g * per_band + k] = total[:, k * features : (k + 1) * features]

        @pl.loop(0, per_band)
        def _(k):
            target = g * per_band + k

            @pl.when(target != expert)
            def _():
                remote(back.at[target], returned.at[expert], bs, br, expert=target).start()

    returned[expert] = back[expert]
    all_of(rows_all.at[pl.ds(0, most)], fs, fr.at[0]).wait_send()
    all_of(product.at[:, pl.ds(0, most)], gs, gr.at[0]).wait_send()
    all_of(returned.at[pl.ds(0, NE - 1)], bs, br).wait_recv()
    both = lax.dot_general(
        mixing[...],
        returned[...].reshape(experts * slots, features),
        (((0,), (0,)), ((), ())),
        preferred_element_type=f32,
    )
    mixture = both[:count] + both[count:]
    final_s[...] = (held_stream[...].astype(f32) + mixture).astype(bf16)
    for k in (1, 3, 2):
        remote(final_s, final_r.at[head], ys, yr, head=lax.rem(head + k, NH)).start()
    final_r[head] = final_s[...]
    all_of(back.at[pl.ds(0, NE - 1)], bs, br).wait_send()
    all_of(final_r.at[pl.ds(0, NH - 1)], ys, yr).wait_recv()
    pieces = [final_r[i].astype(f32).reshape(NZ, sub, features) for i in range(NH)]
    out[...] = jnp.concatenate(
        [pieces[i][r] for r in range(NZ) for i in range(NH)], axis=0
    ).astype(bf16)
    all_of(final_r.at[pl.ds(0, NH - 1)], ys, yr).wait_send()


def on_device(
    tokens, attn_gain, w_query, q_gain, cached_keys, prefix_values, output_weight,
    post_gain, routes, route_gates, w_gate, w_up, w_down,
):
    rows, features = tokens.shape
    width = w_query.shape[1] // NX
    block = rows * w_query.shape[1] // HEAD // NE
    bf16, f32 = jnp.bfloat16, jnp.float32
    keys = cached_keys.shape[0]
    span = rows // NZ
    sub = span // NH
    count = NZ * sub
    halves = 2

    model, ff = w_gate.shape[1:]
    slots = 2 * count // 8
    groups = 2
    bands = 4
    experts = NE * NB
    V = pltpu.VMEM
    return pl.pallas_call(
        layer_kernel,
        out_shape=jax.ShapeDtypeStruct((rows, features), bf16),
        in_specs=[IN_VMEM, IN_VMEM, IN_ANY, IN_VMEM] + [IN_ANY] * 3 + [IN_VMEM] * 3 + [IN_ANY] * 3,
        out_specs=IN_VMEM,
        scratch_shapes=[
            V((NX, rows, features), bf16),
            V((NX, features, width), bf16),
            V((NZ, span, width), f32),
            V((NZ, span, width), f32),
            V((NX, NZ, block, HEAD), bf16),
            V((keys, HEAD), bf16),
            V((keys, HEAD), bf16),
            V((HEAD, keys), bf16),
            V(output_weight.shape, bf16),
            V((keys, NX * block), f32),
            V((NZ, NX, HEAD + LOG_ROWS, block), bf16),
            V((NZ, NX, HEAD + LOG_ROWS, block), bf16),
            V((NZ, HEAD + LOG_ROWS, block), bf16),
            V((NZ, HEAD + LOG_ROWS, block), bf16),
            V((NX, NZ, block, HEAD), bf16),
            V((halves, NH, count // halves, features), f32),
            V((halves, NH, count // halves, features), f32),
            V((NZ, sub, features), f32),
            V((count, features), bf16),
            V((experts * slots, count), bf16),
            V((experts * slots, 2 * count), bf16),
            V((model, ff), bf16),
            V((model, ff), bf16),
            V((ff, model), bf16),
            V((NE, NB * slots, features), bf16),
            V((NE, NB * slots, features), bf16),
            V((NH * NB, NE, slots, features), bf16),
            V((NH * NB * slots, model), bf16),
            V((bands, NH * NB, slots, model // bands), bf16),
            V((bands, NH * NB, slots, model // bands), bf16),
            V((NE, NB * slots, features), bf16),
            V((NE, NB * slots, features), bf16),
            V((count, features), bf16),
            V((NH, count, features), bf16),
            DMA((7,)),
            DMA, DMA, DMA, DMA,
            DMA, DMA,
            DMA, DMA((NZ,)), DMA, DMA((NZ,)),
            DMA, DMA((NZ,)), DMA, DMA,
            DMA, DMA((NZ,)), DMA, DMA((NZ,)),
            DMA, DMA((halves,)),
            DMA, DMA((groups,)), DMA, DMA((groups,)),
            DMA, DMA((bands,)), DMA, DMA, DMA, DMA,
        ],
        compiler_params=pltpu.CompilerParams(
            collective_id=1, has_side_effects=True, vmem_limit_bytes=56 * MIB
        ),
        name="scoring_layer",
    )(
        tokens, attn_gain[None, :], w_query, q_gain[None, :],
        cached_keys, prefix_values, output_weight,
        post_gain.reshape(NE, features), routes.T, route_gates.T,
        w_gate[0], w_up[0], w_down[0],
    )


def solution(mesh):
    placed = (
        P("batch", "expert"),
        P("expert"),
        P("expert", "head"),
        P(),
        P("expert", "head"),
        P("expert", "head"),
        P("head", "expert"),
        P(),
        P("batch", None),
        P("batch", None),
        P(("expert", "batch"), None, "head"),
        P(("expert", "batch"), None, "head"),
        P(("expert", "batch"), "head", None),
    )
    return jax.shard_map(
        on_device, mesh=mesh, in_specs=placed, out_specs=P("batch", "expert"), check_vma=False
    )
```

```python
import functools

import jax
import jax.numpy as jnp
from jax import lax
from jax.experimental import pallas as pl
from jax.experimental.pallas import tpu as pltpu
from jax.sharding import PartitionSpec as P

EPSILON = 1e-06
MIB = 1024 * 1024
NX, NZ, NH, NB = 4, 8, 4, 2
NE = NX * NZ
HEAD = 128
KEY_CHUNK = 256
LOG_ROWS = 16
MESH = pl.DeviceIdType.MESH
IN_VMEM = pl.BlockSpec(memory_space=pltpu.VMEM)
IN_ANY = pl.BlockSpec(memory_space=pl.ANY)
DMA = pltpu.SemaphoreType.DMA
NEAR_FIRST_Z = (1, 7, 2, 6, 3, 5, 4)
NEAR_FIRST_X = (1, 3, 2)
FAR_FIRST_Z = (4, 3, 5, 2, 6, 1, 7)
ATTEND_ORDER = (0, 1, 6, 4, 3, 5, 2, 7)


def remote(src, dst, send_sem, recv_sem, **where):
    return pltpu.make_async_remote_copy(
        src, dst, send_sem, recv_sem, device_id=where, device_id_type=MESH
    )


def here():
    expert = lax.axis_index("expert")
    return expert, expert // NX, lax.rem(expert, NX)


def signal(**where):
    pl.semaphore_signal(
        pltpu.get_barrier_semaphore(), inc=1, device_id=where, device_id_type=MESH
    )


def greet_experts(expert):
    @pl.loop(1, NE)
    def _(k):
        signal(expert=lax.rem(expert + k, NE))


def slot_matrix(routes, gates, experts, group):
    top, count = routes.shape
    names = lax.broadcasted_iota(jnp.int32, (experts, count), 0)
    chosen = jnp.zeros((experts, count), jnp.float32)
    gate = jnp.zeros((experts, count), jnp.float32)
    for k in range(top):
        hit = names == routes[k : k + 1, :]
        chosen = chosen + hit.astype(jnp.float32)
        gate = gate + jnp.where(hit, gates[k : k + 1, :], 0.0)
    earlier = lax.broadcasted_iota(jnp.int32, (count, count), 0)
    later = lax.broadcasted_iota(jnp.int32, (count, count), 1)
    before = ((earlier < later) & (earlier // group == later // group)).astype(jnp.bfloat16)
    rank = jnp.dot(chosen.astype(jnp.bfloat16), before, preferred_element_type=jnp.float32)
    place = chosen * (rank + 1.0)
    slots = 2 * (count // group)
    shape = (experts, slots, count)
    slot = lax.broadcasted_iota(jnp.int32, shape, 1)
    token = lax.broadcasted_iota(jnp.int32, shape, 2)
    wanted = (slot % 2 + 1).astype(jnp.float32)
    hits = (place[:, None, :] == wanted) & (token // group == slot // 2)
    places = hits.astype(jnp.float32)
    return places, places * gate[:, None, :]


def transposed_softmax(queries, keys, values_t, scores):
    count, rows = scores.shape
    chunks = range(0, count, KEY_CHUNK)
    top = jnp.full((8, rows), -jnp.inf, jnp.float32)
    for start in chunks:
        part = lax.dot_general(
            keys[start : start + KEY_CHUNK, :],
            queries,
            (((1,), (1,)), ((), ())),
            preferred_element_type=jnp.float32,
        )
        scores[start : start + KEY_CHUNK, :] = part
        top = jnp.maximum(top, jnp.max(part.reshape(KEY_CHUNK // 8, 8, rows), axis=0))
    peak = jnp.max(top, axis=0, keepdims=True)
    total = jnp.zeros((8, rows), jnp.float32)
    weighted = jnp.zeros((HEAD, rows), jnp.float32)
    for start in chunks:
        probs = jnp.exp(scores[start : start + KEY_CHUNK, :] - peak)
        total = total + jnp.sum(probs.reshape(KEY_CHUNK // 8, 8, rows), axis=0)
        weighted = weighted + jnp.dot(
            values_t[:, start : start + KEY_CHUNK],
            probs.astype(jnp.bfloat16),
            preferred_element_type=jnp.float32,
        )
    total = jnp.sum(total, axis=0, keepdims=True)
    return weighted / total, peak + jnp.log(total)


def with_log(average, log_total):
    rows = average.shape[1]
    high = log_total.astype(jnp.bfloat16).astype(jnp.float32)
    rest = log_total - high
    middle = rest.astype(jnp.bfloat16).astype(jnp.float32)
    low = rest - middle
    place = lax.broadcasted_iota(jnp.int32, (LOG_ROWS, rows), 0)
    tail = jnp.where(place == 0, high, jnp.where(place == 1, middle, low))
    return jnp.concatenate([average, tail], axis=0).astype(jnp.bfloat16)


def merged(blocks):
    logs = []
    for block in blocks:
        tail = block[HEAD : HEAD + LOG_ROWS].astype(jnp.float32)
        logs.append(tail[0:1] + tail[1:2] + tail[2:3])
    top = logs[0]
    for one in logs[1:]:
        top = jnp.maximum(top, one)
    shares = [jnp.exp(one - top) for one in logs]
    total = shares[0]
    for one in shares[1:]:
        total = total + one
    inverse = 1.0 / total
    result = None
    for block, share in zip(blocks, shares):
        term = block[:HEAD].astype(jnp.float32) * (share * inverse)
        result = term if result is None else result + term
    return result, top + jnp.log(total)


def layer_kernel(
    tokens, gain, w_query, q_gain, keys_h, values_h, output_h, post_gain, routes, gates,
    w_gate, w_up, w_down, out,
    scaled, weights, partial, arrived, queries, keys, values, values_t, output_weight, scores,
    average_s, average_x, merged_s, merged_z, attended, part, part_r, ordered, held_stream,
    places, mixing, gate_v, up_v, down_v, outgoing, stage, rows_all, normed, product, parts,
    back, returned, final_s, final_r,
    load, ts, tr, ws, wr, ps, pr, qs, qr, fqs, fqr,
    xas, xar, zas, zar, ms, mr, fms, fmr, hs, hr,
    es, er, fs, fr, gs, gr, bs, br, ys, yr,
):
    expert, z, x = here()
    head = lax.axis_index("head")
    core = lax.axis_index("batch")
    f32, bf16 = jnp.float32, jnp.bfloat16
    width = w_query.shape[1] // NX
    rows, features = tokens.shape
    block = queries.shape[2]
    span = rows // NZ
    heads_here = width // HEAD
    sub = span // NH
    count = NZ * sub
    others = [(i, j) for j in range(NB) for i in range(NH) if (i, j) != (0, 0)]

    def columns(owner):
        return pl.ds(pl.multiple_of(owner * width, width), width)

    own_weights = pltpu.make_async_copy(w_query.at[:, columns(x)], weights.at[x], load.at[0])
    own_weights.start()
    load_keys = pltpu.make_async_copy(keys_h, keys, load.at[1])
    load_values = pltpu.make_async_copy(values_h, values, load.at[2])
    load_output = pltpu.make_async_copy(output_h, output_weight, load.at[3])
    load_gate = pltpu.make_async_copy(w_gate, gate_v, load.at[4])
    load_up = pltpu.make_async_copy(w_up, up_v, load.at[5])
    load_down = pltpu.make_async_copy(w_down, down_v, load.at[6])

    @pl.loop(1, NE)
    def _(k):
        signal(expert=lax.rem(expert + k, NE))

    for i, j in others:
        signal(head=lax.rem(head + i, NH), batch=lax.rem(core + j, NB))
    scaled[x] = (tokens[...].astype(f32) * gain[...].astype(f32)).astype(bf16)
    pl.semaphore_wait(pltpu.get_barrier_semaphore(), NE - 1 + len(others))

    def weight_copy(owner, source):
        return remote(
            w_query.at[:, columns(owner)], weights.at[source], ws, wr, expert=z * NX + owner
        )

    def token_copy(target, source):
        return remote(scaled.at[source], scaled.at[source], ts, tr, expert=z * NX + target)

    def sum_copy(target, source):
        return remote(
            partial.at[target], arrived.at[source], ps, pr, expert=target * NX + x
        )

    def all_of(ref, send_sem, recv_sem):
        return remote(ref, ref, send_sem, recv_sem, expert=expert)

    for k in NEAR_FIRST_X:
        target = lax.rem(x + k, NX)
        token_copy(target, x).start()
        weight_copy(target, x).start()
    load_keys.start()
    load_values.start()
    load_output.start()
    own_weights.wait()
    all_of(scaled.at[pl.ds(0, NX - 1)], ts, tr).wait_recv()
    all_of(weights.at[pl.ds(0, NX - 1)], ws, wr).wait_recv()
    left = jnp.concatenate([scaled[i] for i in range(NX)], axis=1)
    right = weights[...].reshape(NX * features, width)
    partial[...] = jnp.dot(left, right, preferred_element_type=f32).reshape(NZ, span, width)
    for k in FAR_FIRST_Z:
        sum_copy(lax.rem(z + k, NZ), z).start()
    arrived[z] = partial[z]
    load_gate.start()
    load_up.start()
    load_down.start()
    slots = 2 * count // 8
    experts = NE * NB
    token = lax.broadcasted_iota(jnp.int32, (rows, count), 0)
    owned = lax.broadcasted_iota(jnp.int32, (rows, count), 1)
    mine = (token == owned // sub * span + head * sub + owned % sub).astype(f32)

    def own(table):
        return jnp.dot(
            table, mine, precision=lax.Precision.HIGHEST, preferred_element_type=f32
        )

    own_routes = own(routes[...].astype(f32)).astype(jnp.int32)
    chosen, weighted = slot_matrix(own_routes, own(gates[...]), experts, 8)
    places[...] = chosen.reshape(experts * slots, count).astype(bf16)
    flat = weighted.reshape(experts * slots, count)
    high = flat.astype(bf16)
    low = flat - high.astype(f32)
    mixing[...] = jnp.concatenate([high.astype(f32), low], axis=1).T.astype(bf16)
    load_values.wait()
    for i in range(0, values.shape[0], 128):
        values_t[:, i : i + 128] = values[i : i + 128, :].astype(f32).T.astype(bf16)
    all_of(scaled.at[pl.ds(0, NX - 1)], ts, tr).wait_send()
    all_of(weights.at[pl.ds(0, NX - 1)], ws, wr).wait_send()
    load_keys.wait()
    load_output.wait()
    all_of(arrived.at[pl.ds(0, NZ - 1)], ps, pr).wait_recv()
    total = arrived[0]
    for i in range(1, NZ):
        total = total + arrived[i]
    factor = q_gain[...].astype(f32) / jnp.sqrt(f32(HEAD))
    heads = []
    for h in range(heads_here):
        one = total[:, h * HEAD : (h + 1) * HEAD]
        mean = jnp.mean(one * one, axis=-1, keepdims=True)
        heads.append(one * lax.rsqrt(mean + EPSILON) * factor)
    queries[x, z] = jnp.concatenate(heads, axis=0).astype(bf16)

    def at_step(n):
        near = (n + 1) // 2
        return lax.rem(z + jnp.where(n % 2 == 1, near, NZ - near), NZ)

    def at_turn(n):
        offset = ATTEND_ORDER[NZ - 1]
        for i in range(NZ - 1):
            offset = jnp.where(n == i, ATTEND_ORDER[i], offset)
        return lax.rem(z + offset, NZ)

    def spread(blocks, send_sem, recv_sem):
        for k in NEAR_FIRST_Z:
            remote(
                blocks.at[x, z], blocks.at[x, z], send_sem, recv_sem.at[z],
                expert=lax.rem(z + k, NZ) * NX + x,
            ).start()

    def pass_on(blocks, z_sems, send_sem, recv_sem, n, order):
        r = order(n)
        block = blocks.at[x, r]

        @pl.when(n >= 1)
        def _():
            all_of(block, z_sems[0], z_sems[1].at[r]).wait_recv()

        for k in NEAR_FIRST_X:
            remote(
                block, block, send_sem, recv_sem.at[r], expert=z * NX + lax.rem(x + k, NX)
            ).start()

    def passed(blocks, send_sem, recv_sem, n, order):
        r = order(n)
        return all_of(blocks.at[pl.ds(0, NX - 1), r], send_sem, recv_sem.at[r])

    def attend(n):
        r = at_turn(n)
        here_rows = queries[:, r].reshape(NX * block, HEAD)
        average, log_total = transposed_softmax(here_rows, keys, values_t, scores)
        both = with_log(average, log_total)
        for i in range(NX):
            average_s[r, i] = both[:, i * block : (i + 1) * block]
        for k in NEAR_FIRST_X:
            target = lax.rem(x + k, NX)
            remote(
                average_s.at[r, target], average_x.at[r, x], xas, xar.at[r],
                expert=z * NX + target,
            ).start()
        average_x[r, x] = average_s[r, x]

    def merge_x(n):
        r = at_turn(n)
        all_of(average_x.at[r, pl.ds(0, NX - 1)], xas, xar.at[r]).wait_recv()
        average, log_total = merged([average_x[r, i] for i in range(NX)])
        merged_s[r] = with_log(average, log_total)

        @pl.when(n == 0)
        def _():
            merged_z[z] = merged_s[z]

        @pl.when(n >= 1)
        def _():
            remote(merged_s.at[r], merged_z.at[z], zas, zar, expert=r * NX + x).start()

    parts_of_z = 2
    per_part = NZ // parts_of_z

    def project(which):
        tall = []
        for n in range(which * per_part, (which + 1) * per_part):
            passed(attended, fms, fmr, n, at_step).wait_recv()
            r = at_step(n)
            tall.append(
                jnp.concatenate(
                    [
                        attended[i, r, j * span : (j + 1) * span, :]
                        for i in range(NX)
                        for j in range(heads_here)
                    ],
                    axis=1,
                )
            )
        left = jnp.concatenate(tall, axis=0)
        made = jnp.dot(left, output_weight[...], preferred_element_type=f32)
        made = made.reshape(per_part, NH, sub, features)
        for i in range(NH):
            part[which, i] = made[:, i].reshape(per_part * sub, features)
        for k in (1, 3, 2):
            target = lax.rem(head + k, NH)
            remote(
                part.at[which, target], part_r.at[which, head], hs, hr.at[which], head=target
            ).start()
        part_r[which, head] = part[which, head]

    groups = er.shape[0]
    per_group = NE // groups
    own_group = expert // per_group
    me_hb = head * NB + core
    most = len(others)

    def group_of(step):
        return lax.rem(own_group + step, groups)

    def members(g):
        return pl.ds(g * per_group, per_group)

    def half(owner):
        return pl.ds(pl.multiple_of(owner * slots, slots), slots)

    def target_of(i, j):
        return lax.rem(head + i, NH), lax.rem(core + j, NB)

    def dispatch():
        for which in range(parts_of_z):
            all_of(part_r.at[which, pl.ds(0, NH - 1)], hs, hr.at[which]).wait_recv()
            summed = part_r[which, 0]
            for i in range(1, NH):
                summed = summed + part_r[which, i]
            summed = summed.reshape(per_part, sub, features)
            for n in range(per_part):
                ordered[at_step(which * per_part + n)] = summed[n]
        resid = tokens[...].astype(f32).reshape(NZ, NH, sub, features)
        mine = jnp.zeros((NZ, sub, features), f32)
        for i in range(NH):
            mine = jnp.where(head == i, resid[:, i], mine)
        held_stream[...] = (mine + ordered[...]).reshape(count, features).astype(bf16)
        picked = jnp.dot(places[...], held_stream[...], preferred_element_type=f32)
        outgoing[...] = picked.astype(bf16).reshape(NE, NB * slots, features)

        @pl.loop(0, NE - 1)
        def _(n):
            step = (n + 1) // 2
            k = NE // 2 + jnp.where(n % 2 == 1, step, -step)
            target = lax.rem(expert + k, NE)
            remote(
                outgoing.at[target], stage.at[expert], es, er.at[own_group], expert=target
            ).start()

        stage[expert] = outgoing[expert]

    def forward():
        @pl.loop(0, groups)
        def _(step):
            g = group_of(step)

            @pl.when(step == 0)
            def _():
                few = stage.at[pl.ds(0, per_group - 1)]
                all_of(few, es, er.at[g]).wait_recv()

            @pl.when(step != 0)
            def _():
                all_of(stage.at[members(g)], es, er.at[g]).wait_recv()

            for i, j in others:
                to_head, to_core = target_of(i, j)
                remote(
                    stage.at[members(g), half(to_core)],
                    rows_all.at[me_hb, members(g)],
                    fs,
                    fr.at[g],
                    head=to_head,
                    batch=to_core,
                ).start()
            rows_all[me_hb, members(g)] = stage[members(g), half(core)]

    ahead = 2
    spread(queries, qs, qr)
    for n in range(ahead):
        pass_on(queries, (qs, qr), fqs, fqr, n, at_turn)

    @pl.loop(0, NZ)
    def _(n):
        @pl.when(n + ahead < NZ)
        def _():
            pass_on(queries, (qs, qr), fqs, fqr, n + ahead, at_turn)

        passed(queries, fqs, fqr, n, at_turn).wait_recv()
        attend(n)

        @pl.when(n >= 2)
        def _():
            merge_x(n - 2)

    merge_x(NZ - 2)
    merge_x(NZ - 1)
    all_of(merged_z.at[pl.ds(0, NZ - 1)], zas, zar).wait_recv()
    average, _ = merged([merged_z[i] for i in range(NZ)])
    attended[x, z] = average.T.astype(bf16)
    spread(attended, ms, mr)
    for n in range(NZ):
        pass_on(attended, (ms, mr), fms, fmr, n, at_step)
    for which in range(parts_of_z):
        project(which)
    dispatch()
    load_gate.wait()
    load_up.wait()
    load_down.wait()
    all_of(queries.at[0, pl.ds(0, NZ - 1)], qs, qr.at[0]).wait_send()
    all_of(queries.at[pl.ds(0, NX - 1)], fqs, fqr.at[0]).wait_send()
    all_of(average_s.at[:, pl.ds(0, NX - 1)], xas, xar.at[0]).wait_send()
    all_of(arrived.at[pl.ds(0, NZ - 1)], ps, pr).wait_send()
    all_of(merged_s.at[pl.ds(0, NZ - 1)], zas, zar).wait_send()
    all_of(attended.at[0, pl.ds(0, NZ - 1)], ms, mr.at[0]).wait_send()
    all_of(attended.at[pl.ds(0, NX - 1)], fms, fmr.at[0]).wait_send()
    all_of(part.at[:, pl.ds(0, NH - 1)], hs, hr.at[0]).wait_send()
    forward()
    all_of(outgoing.at[pl.ds(0, NE - 1)], es, er.at[0]).wait_send()

    held = NH * NB * slots
    square = jnp.zeros((held, features), f32)
    for g in range(groups):
        for e in range(g * per_group, (g + 1) * per_group):
            if e == g * per_group:
                all_of(rows_all.at[pl.ds(0, most), members(g)], fs, fr.at[g]).wait_recv()
            wide = rows_all[:, e].reshape(held, features).astype(f32)
            square = square + wide * wide
    mean = jnp.sum(square, axis=1, keepdims=True) * (1.0 / (NE * features))
    scale = lax.rsqrt(mean + EPSILON)
    for e in range(NE):
        wide = rows_all[:, e].reshape(held, features).astype(f32)
        normed[:, e * features : (e + 1) * features] = (
            wide * scale * post_gain[e : e + 1, :].astype(f32)
        ).astype(bf16)
    gate_part = jnp.dot(normed[...], gate_v[...], preferred_element_type=f32)
    up_part = jnp.dot(normed[...], up_v[...], preferred_element_type=f32)
    hidden = (gate_part / (1.0 + jnp.exp(-gate_part)) * up_part).astype(bf16)
    reach = parts.shape[-1]
    bands = parts.shape[0]
    per_band = NE // bands

    own_band = expert // per_band
    band_order = [lax.rem(own_band + i, bands) for i in (2, 1, 3, 0)]
    for g in band_order:
        lanes = pl.ds(pl.multiple_of(g * reach, reach), reach)
        made = jnp.dot(hidden, down_v[:, lanes], preferred_element_type=f32)
        product[g] = made.astype(bf16).reshape(NH * NB, slots, reach)
        for i, j in others:
            to_head, to_core = target_of(i, j)
            remote(
                product.at[g, to_head * NB + to_core],
                parts.at[g, me_hb],
                gs,
                gr.at[g],
                head=to_head,
                batch=to_core,
            ).start()
        parts[g, me_hb] = product[g, me_hb]

    for g in band_order:
        all_of(parts.at[g, pl.ds(0, most)], gs, gr.at[g]).wait_recv()
        total = parts[g, pl.ds(0, NB)].astype(f32)
        for i in range(1, NH):
            total = total + parts[g, pl.ds(i * NB, NB)].astype(f32)
        total = total.reshape(NB * slots, reach).astype(bf16)
        for k in range(per_band):
            back[g * per_band + k] = total[:, k * features : (k + 1) * features]

        @pl.loop(0, per_band)
        def _(k):
            target = g * per_band + k

            @pl.when(target != expert)
            def _():
                remote(back.at[target], returned.at[expert], bs, br, expert=target).start()

    returned[expert] = back[expert]
    all_of(rows_all.at[pl.ds(0, most)], fs, fr.at[0]).wait_send()
    all_of(product.at[:, pl.ds(0, most)], gs, gr.at[0]).wait_send()
    all_of(returned.at[pl.ds(0, NE - 1)], bs, br).wait_recv()
    both = jnp.dot(
        mixing[...],
        returned[...].reshape(experts * slots, features),
        preferred_element_type=f32,
    )
    mixture = both[:count] + both[count:]
    final_s[...] = (held_stream[...].astype(f32) + mixture).astype(bf16)
    for k in (1, 3, 2):
        remote(final_s, final_r.at[head], ys, yr, head=lax.rem(head + k, NH)).start()
    final_r[head] = final_s[...]
    all_of(back.at[pl.ds(0, NE - 1)], bs, br).wait_send()
    all_of(final_r.at[pl.ds(0, NH - 1)], ys, yr).wait_recv()
    pieces = [final_r[i].astype(f32).reshape(NZ, sub, features) for i in range(NH)]
    out[...] = jnp.concatenate(
        [pieces[i][r] for r in range(NZ) for i in range(NH)], axis=0
    ).astype(bf16)
    all_of(final_r.at[pl.ds(0, NH - 1)], ys, yr).wait_send()


def on_device(
    tokens, attn_gain, w_query, q_gain, cached_keys, prefix_values, output_weight,
    post_gain, routes, route_gates, w_gate, w_up, w_down,
):
    rows, features = tokens.shape
    width = w_query.shape[1] // NX
    block = rows * w_query.shape[1] // HEAD // NE
    bf16, f32 = jnp.bfloat16, jnp.float32
    keys = cached_keys.shape[0]
    span = rows // NZ
    sub = span // NH
    count = NZ * sub
    halves = 2

    model, ff = w_gate.shape[1:]
    slots = 2 * count // 8
    groups = 2
    bands = 4
    experts = NE * NB
    V = pltpu.VMEM
    return pl.pallas_call(
        layer_kernel,
        out_shape=jax.ShapeDtypeStruct((rows, features), bf16),
        in_specs=[IN_VMEM, IN_VMEM, IN_ANY, IN_VMEM] + [IN_ANY] * 3 + [IN_VMEM] * 3 + [IN_ANY] * 3,
        out_specs=IN_VMEM,
        scratch_shapes=[
            V((NX, rows, features), bf16),
            V((NX, features, width), bf16),
            V((NZ, span, width), f32),
            V((NZ, span, width), f32),
            V((NX, NZ, block, HEAD), bf16),
            V((keys, HEAD), bf16),
            V((keys, HEAD), bf16),
            V((HEAD, keys), bf16),
            V(output_weight.shape, bf16),
            V((keys, NX * block), f32),
            V((NZ, NX, HEAD + LOG_ROWS, block), bf16),
            V((NZ, NX, HEAD + LOG_ROWS, block), bf16),
            V((NZ, HEAD + LOG_ROWS, block), bf16),
            V((NZ, HEAD + LOG_ROWS, block), bf16),
            V((NX, NZ, block, HEAD), bf16),
            V((halves, NH, count // halves, features), f32),
            V((halves, NH, count // halves, features), f32),
            V((NZ, sub, features), f32),
            V((count, features), bf16),
            V((experts * slots, count), bf16),
            V((2 * count, experts * slots), bf16),
            V((model, ff), bf16),
            V((model, ff), bf16),
            V((ff, model), bf16),
            V((NE, NB * slots, features), bf16),
            V((NE, NB * slots, features), bf16),
            V((NH * NB, NE, slots, features), bf16),
            V((NH * NB * slots, model), bf16),
            V((bands, NH * NB, slots, model // bands), bf16),
            V((bands, NH * NB, slots, model // bands), bf16),
            V((NE, NB * slots, features), bf16),
            V((NE, NB * slots, features), bf16),
            V((count, features), bf16),
            V((NH, count, features), bf16),
            DMA((7,)),
            DMA, DMA, DMA, DMA,
            DMA, DMA,
            DMA, DMA((NZ,)), DMA, DMA((NZ,)),
            DMA, DMA((NZ,)), DMA, DMA,
            DMA, DMA((NZ,)), DMA, DMA((NZ,)),
            DMA, DMA((halves,)),
            DMA, DMA((groups,)), DMA, DMA((groups,)),
            DMA, DMA((bands,)), DMA, DMA, DMA, DMA,
        ],
        compiler_params=pltpu.CompilerParams(
            collective_id=1, has_side_effects=True, vmem_limit_bytes=56 * MIB
        ),
        name="scoring_layer",
    )(
        tokens, attn_gain[None, :], w_query, q_gain[None, :],
        cached_keys, prefix_values, output_weight,
        post_gain.reshape(NE, features), routes.T, route_gates.T,
        w_gate[0], w_up[0], w_down[0],
    )


def solution(mesh):
    placed = (
        P("batch", "expert"),
        P("expert"),
        P("expert", "head"),
        P(),
        P("expert", "head"),
        P("expert", "head"),
        P("head", "expert"),
        P(),
        P("batch", None),
        P("batch", None),
        P(("expert", "batch"), None, "head"),
        P(("expert", "batch"), None, "head"),
        P(("expert", "batch"), "head", None),
    )
    return jax.shard_map(
        on_device, mesh=mesh, in_specs=placed, out_specs=P("batch", "expert"), check_vma=False
    )
```

```python
import functools

import jax
import jax.numpy as jnp
from jax import lax
from jax.experimental import pallas as pl
from jax.experimental.pallas import tpu as pltpu
from jax.sharding import PartitionSpec as P

EPSILON = 1e-06
MIB = 1024 * 1024
NX, NZ, NH, NB = 4, 8, 4, 2
NE = NX * NZ
HEAD = 128
KEY_CHUNK = 256
LOG_ROWS = 16
MESH = pl.DeviceIdType.MESH
IN_VMEM = pl.BlockSpec(memory_space=pltpu.VMEM)
IN_ANY = pl.BlockSpec(memory_space=pl.ANY)
DMA = pltpu.SemaphoreType.DMA
NEAR_FIRST_Z = (1, 7, 2, 6, 3, 5, 4)
NEAR_FIRST_X = (1, 3, 2)
FAR_FIRST_Z = (4, 3, 5, 2, 6, 1, 7)
ATTEND_ORDER = (0, 1, 6, 4, 3, 5, 2, 7)


def remote(src, dst, send_sem, recv_sem, **where):
    return pltpu.make_async_remote_copy(
        src, dst, send_sem, recv_sem, device_id=where, device_id_type=MESH
    )


def here():
    expert = lax.axis_index("expert")
    return expert, expert // NX, lax.rem(expert, NX)


def signal(**where):
    pl.semaphore_signal(
        pltpu.get_barrier_semaphore(), inc=1, device_id=where, device_id_type=MESH
    )


def greet_experts(expert):
    @pl.loop(1, NE)
    def _(k):
        signal(expert=lax.rem(expert + k, NE))


def slot_matrix(routes, gates, experts, group):
    top, count = routes.shape
    names = lax.broadcasted_iota(jnp.int32, (experts, count), 0)
    chosen = jnp.zeros((experts, count), jnp.float32)
    gate = jnp.zeros((experts, count), jnp.float32)
    for k in range(top):
        hit = names == routes[k : k + 1, :]
        chosen = chosen + hit.astype(jnp.float32)
        gate = gate + jnp.where(hit, gates[k : k + 1, :], 0.0)
    earlier = lax.broadcasted_iota(jnp.int32, (count, count), 0)
    later = lax.broadcasted_iota(jnp.int32, (count, count), 1)
    before = ((earlier < later) & (earlier // group == later // group)).astype(jnp.bfloat16)
    rank = jnp.dot(chosen.astype(jnp.bfloat16), before, preferred_element_type=jnp.float32)
    place = chosen * (rank + 1.0)
    slots = 2 * (count // group)
    shape = (experts, slots, count)
    slot = lax.broadcasted_iota(jnp.int32, shape, 1)
    token = lax.broadcasted_iota(jnp.int32, shape, 2)
    wanted = (slot % 2 + 1).astype(jnp.float32)
    hits = (place[:, None, :] == wanted) & (token // group == slot // 2)
    places = hits.astype(jnp.float32)
    return places, places * gate[:, None, :]


def transposed_softmax(queries, keys, values_t, scores):
    count, rows = scores.shape
    chunks = range(0, count, KEY_CHUNK)
    top = jnp.full((8, rows), -jnp.inf, jnp.float32)
    for start in chunks:
        part = lax.dot_general(
            keys[start : start + KEY_CHUNK, :],
            queries,
            (((1,), (1,)), ((), ())),
            preferred_element_type=jnp.float32,
        )
        scores[start : start + KEY_CHUNK, :] = part
        top = jnp.maximum(top, jnp.max(part.reshape(KEY_CHUNK // 8, 8, rows), axis=0))
    peak = jnp.max(top, axis=0, keepdims=True)
    total = jnp.zeros((8, rows), jnp.float32)
    weighted = jnp.zeros((HEAD, rows), jnp.float32)
    for start in chunks:
        probs = jnp.exp(scores[start : start + KEY_CHUNK, :] - peak)
        total = total + jnp.sum(probs.reshape(KEY_CHUNK // 8, 8, rows), axis=0)
        weighted = weighted + jnp.dot(
            values_t[:, start : start + KEY_CHUNK],
            probs.astype(jnp.bfloat16),
            preferred_element_type=jnp.float32,
        )
    total = jnp.sum(total, axis=0, keepdims=True)
    return weighted / total, peak + jnp.log(total)


def with_log(average, log_total):
    rows = average.shape[1]
    high = log_total.astype(jnp.bfloat16).astype(jnp.float32)
    rest = log_total - high
    middle = rest.astype(jnp.bfloat16).astype(jnp.float32)
    low = rest - middle
    place = lax.broadcasted_iota(jnp.int32, (LOG_ROWS, rows), 0)
    tail = jnp.where(place == 0, high, jnp.where(place == 1, middle, low))
    return jnp.concatenate([average, tail], axis=0).astype(jnp.bfloat16)


def merged(blocks):
    logs = []
    for block in blocks:
        tail = block[HEAD : HEAD + LOG_ROWS].astype(jnp.float32)
        logs.append(tail[0:1] + tail[1:2] + tail[2:3])
    top = logs[0]
    for one in logs[1:]:
        top = jnp.maximum(top, one)
    shares = [jnp.exp(one - top) for one in logs]
    total = shares[0]
    for one in shares[1:]:
        total = total + one
    inverse = 1.0 / total
    result = None
    for block, share in zip(blocks, shares):
        term = block[:HEAD].astype(jnp.float32) * (share * inverse)
        result = term if result is None else result + term
    return result, top + jnp.log(total)


def layer_kernel(
    tokens, gain, w_query, q_gain, keys_h, values_h, output_h, post_gain, routes, gates,
    w_gate, w_up, w_down, out,
    scaled, weights, partial, arrived, queries, keys, values, values_t, output_weight, scores,
    average_s, average_x, merged_s, merged_z, attended, part, part_r, ordered, held_stream,
    places, mixing, gate_v, up_v, down_v, outgoing, stage, rows_all, normed, product, parts,
    back, returned, final_s, final_r,
    load, ts, tr, ws, wr, cs, cr, ps, pr, qs, qr, fqs, fqr,
    xas, xar, zas, zar, ms, mr, fms, fmr, hs, hr,
    es, er, fs, fr, gs, gr, bs, br, ys, yr,
):
    expert, z, x = here()
    head = lax.axis_index("head")
    core = lax.axis_index("batch")
    f32, bf16 = jnp.float32, jnp.bfloat16
    width = w_query.shape[1] // NX
    rows, features = tokens.shape
    block = queries.shape[2]
    span = rows // NZ
    heads_here = width // HEAD
    sub = span // NH
    count = NZ * sub
    others = [(i, j) for j in range(NB) for i in range(NH) if (i, j) != (0, 0)]

    def columns(owner):
        return pl.ds(pl.multiple_of(owner * width, width), width)

    own_weights = pltpu.make_async_copy(w_query.at[:, columns(x)], weights.at[x], load.at[0])
    own_weights.start()
    load_keys = pltpu.make_async_copy(keys_h, keys, load.at[1])
    load_values = pltpu.make_async_copy(values_h, values, load.at[2])
    load_output = pltpu.make_async_copy(output_h, output_weight, load.at[3])
    load_gate = pltpu.make_async_copy(w_gate, gate_v, load.at[4])
    load_up = pltpu.make_async_copy(w_up, up_v, load.at[5])
    load_down = pltpu.make_async_copy(w_down, down_v, load.at[6])

    @pl.loop(1, NE)
    def _(k):
        signal(expert=lax.rem(expert + k, NE))

    for i, j in others:
        signal(head=lax.rem(head + i, NH), batch=lax.rem(core + j, NB))
    scaled[x] = (tokens[...].astype(f32) * gain[...].astype(f32)).astype(bf16)
    pl.semaphore_wait(pltpu.get_barrier_semaphore(), NE - 1 + len(others))

    half_features = features // NB
    my_half = pl.ds(pl.multiple_of(core * half_features, half_features), half_features)

    def weight_copy(owner, source):
        return remote(
            w_query.at[my_half, columns(owner)], weights.at[source, my_half], ws, wr,
            expert=z * NX + owner,
        )

    def core_copy(source):
        return remote(
            weights.at[source, my_half], weights.at[source, my_half], cs, cr, batch=1 - core
        )

    def token_copy(target, source):
        return remote(scaled.at[source], scaled.at[source], ts, tr, expert=z * NX + target)

    def sum_copy(target, source):
        return remote(
            partial.at[target], arrived.at[source], ps, pr, expert=target * NX + x
        )

    def all_of(ref, send_sem, recv_sem):
        return remote(ref, ref, send_sem, recv_sem, expert=expert)

    for k in NEAR_FIRST_X:
        target = lax.rem(x + k, NX)
        weight_copy(target, x).start()
    for k in NEAR_FIRST_X:
        token_copy(lax.rem(x + k, NX), x).start()
    load_keys.start()
    load_values.start()
    load_output.start()
    own_weights.wait()
    some = weights.at[pl.ds(0, NX - 1), pl.ds(0, half_features)]
    all_of(some, ws, wr).wait_recv()
    for k in NEAR_FIRST_X:
        core_copy(lax.rem(x + k, NX)).start()
    all_of(scaled.at[pl.ds(0, NX - 1)], ts, tr).wait_recv()
    all_of(some, cs, cr).wait_recv()
    left = jnp.concatenate([scaled[i] for i in range(NX)], axis=1)
    right = weights[...].reshape(NX * features, width)
    partial[...] = jnp.dot(left, right, preferred_element_type=f32).reshape(NZ, span, width)
    for k in FAR_FIRST_Z:
        sum_copy(lax.rem(z + k, NZ), z).start()
    arrived[z] = partial[z]
    load_gate.start()
    load_up.start()
    load_down.start()
    slots = 2 * count // 8
    experts = NE * NB
    token = lax.broadcasted_iota(jnp.int32, (rows, count), 0)
    owned = lax.broadcasted_iota(jnp.int32, (rows, count), 1)
    mine = (token == owned // sub * span + head * sub + owned % sub).astype(f32)

    def own(table):
        return jnp.dot(
            table, mine, precision=lax.Precision.HIGHEST, preferred_element_type=f32
        )

    own_routes = own(routes[...].astype(f32)).astype(jnp.int32)
    chosen, weighted = slot_matrix(own_routes, own(gates[...]), experts, 8)
    places[...] = chosen.reshape(experts * slots, count).astype(bf16)
    flat = weighted.reshape(experts * slots, count)
    high = flat.astype(bf16)
    low = flat - high.astype(f32)
    mixing[...] = jnp.concatenate([high.astype(f32), low], axis=1).T.astype(bf16)
    load_values.wait()
    for i in range(0, values.shape[0], 128):
        values_t[:, i : i + 128] = values[i : i + 128, :].astype(f32).T.astype(bf16)
    all_of(scaled.at[pl.ds(0, NX - 1)], ts, tr).wait_send()
    all_of(some, ws, wr).wait_send()
    all_of(some, cs, cr).wait_send()
    load_keys.wait()
    load_output.wait()
    all_of(arrived.at[pl.ds(0, NZ - 1)], ps, pr).wait_recv()
    total = arrived[0]
    for i in range(1, NZ):
        total = total + arrived[i]
    factor = q_gain[...].astype(f32) / jnp.sqrt(f32(HEAD))
    heads = []
    for h in range(heads_here):
        one = total[:, h * HEAD : (h + 1) * HEAD]
        mean = jnp.mean(one * one, axis=-1, keepdims=True)
        heads.append(one * lax.rsqrt(mean + EPSILON) * factor)
    queries[x, z] = jnp.concatenate(heads, axis=0).astype(bf16)

    def at_step(n):
        near = (n + 1) // 2
        return lax.rem(z + jnp.where(n % 2 == 1, near, NZ - near), NZ)

    def at_turn(n):
        offset = ATTEND_ORDER[NZ - 1]
        for i in range(NZ - 1):
            offset = jnp.where(n == i, ATTEND_ORDER[i], offset)
        return lax.rem(z + offset, NZ)

    def spread(blocks, send_sem, recv_sem):
        for k in NEAR_FIRST_Z:
            remote(
                blocks.at[x, z], blocks.at[x, z], send_sem, recv_sem.at[z],
                expert=lax.rem(z + k, NZ) * NX + x,
            ).start()

    def pass_on(blocks, z_sems, send_sem, recv_sem, n, order):
        r = order(n)
        block = blocks.at[x, r]

        @pl.when(n >= 1)
        def _():
            all_of(block, z_sems[0], z_sems[1].at[r]).wait_recv()

        for k in NEAR_FIRST_X:
            remote(
                block, block, send_sem, recv_sem.at[r], expert=z * NX + lax.rem(x + k, NX)
            ).start()

    def passed(blocks, send_sem, recv_sem, n, order):
        r = order(n)
        return all_of(blocks.at[pl.ds(0, NX - 1), r], send_sem, recv_sem.at[r])

    def attend(n):
        r = at_turn(n)
        here_rows = queries[:, r].reshape(NX * block, HEAD)
        average, log_total = transposed_softmax(here_rows, keys, values_t, scores)
        both = with_log(average, log_total)
        for i in range(NX):
            average_s[r, i] = both[:, i * block : (i + 1) * block]
        for k in NEAR_FIRST_X:
            target = lax.rem(x + k, NX)
            remote(
                average_s.at[r, target], average_x.at[r, x], xas, xar.at[r],
                expert=z * NX + target,
            ).start()
        average_x[r, x] = average_s[r, x]

    def merge_x(n):
        r = at_turn(n)
        all_of(average_x.at[r, pl.ds(0, NX - 1)], xas, xar.at[r]).wait_recv()
        average, log_total = merged([average_x[r, i] for i in range(NX)])
        merged_s[r] = with_log(average, log_total)

        @pl.when(n == 0)
        def _():
            merged_z[z] = merged_s[z]

        @pl.when(n >= 1)
        def _():
            remote(merged_s.at[r], merged_z.at[z], zas, zar, expert=r * NX + x).start()

    parts_of_z = 2
    per_part = NZ // parts_of_z

    def project(which):
        tall = []
        for n in range(which * per_part, (which + 1) * per_part):
            passed(attended, fms, fmr, n, at_step).wait_recv()
            r = at_step(n)
            tall.append(
                jnp.concatenate(
                    [
                        attended[i, r, j * span : (j + 1) * span, :]
                        for i in range(NX)
                        for j in range(heads_here)
                    ],
                    axis=1,
                )
            )
        left = jnp.concatenate(tall, axis=0)
        made = jnp.dot(left, output_weight[...], preferred_element_type=f32)
        made = made.reshape(per_part, NH, sub, features)
        for i in range(NH):
            part[which, i] = made[:, i].reshape(per_part * sub, features)
        for k in (1, 3, 2):
            target = lax.rem(head + k, NH)
            remote(
                part.at[which, target], part_r.at[which, head], hs, hr.at[which], head=target
            ).start()
        part_r[which, head] = part[which, head]

    groups = er.shape[0]
    per_group = NE // groups
    own_group = expert // per_group
    me_hb = head * NB + core
    most = len(others)

    def group_of(step):
        return lax.rem(own_group + step, groups)

    def members(g):
        return pl.ds(g * per_group, per_group)

    def half(owner):
        return pl.ds(pl.multiple_of(owner * slots, slots), slots)

    def target_of(i, j):
        return lax.rem(head + i, NH), lax.rem(core + j, NB)

    def dispatch():
        for which in range(parts_of_z):
            all_of(part_r.at[which, pl.ds(0, NH - 1)], hs, hr.at[which]).wait_recv()
            summed = part_r[which, 0]
            for i in range(1, NH):
                summed = summed + part_r[which, i]
            summed = summed.reshape(per_part, sub, features)
            for n in range(per_part):
                ordered[at_step(which * per_part + n)] = summed[n]
        resid = tokens[...].astype(f32).reshape(NZ, NH, sub, features)
        mine = jnp.zeros((NZ, sub, features), f32)
        for i in range(NH):
            mine = jnp.where(head == i, resid[:, i], mine)
        held_stream[...] = (mine + ordered[...]).reshape(count, features).astype(bf16)
        picked = jnp.dot(places[...], held_stream[...], preferred_element_type=f32)
        outgoing[...] = picked.astype(bf16).reshape(NE, NB * slots, features)

        @pl.loop(0, NE - 1)
        def _(n):
            step = (n + 1) // 2
            k = NE // 2 + jnp.where(n % 2 == 1, step, -step)
            target = lax.rem(expert + k, NE)
            remote(
                outgoing.at[target], stage.at[expert], es, er.at[own_group], expert=target
            ).start()

        stage[expert] = outgoing[expert]

    def forward():
        @pl.loop(0, groups)
        def _(step):
            g = group_of(step)

            @pl.when(step == 0)
            def _():
                few = stage.at[pl.ds(0, per_group - 1)]
                all_of(few, es, er.at[g]).wait_recv()

            @pl.when(step != 0)
            def _():
                all_of(stage.at[members(g)], es, er.at[g]).wait_recv()

            for i, j in others:
                to_head, to_core = target_of(i, j)
                remote(
                    stage.at[members(g), half(to_core)],
                    rows_all.at[me_hb, members(g)],
                    fs,
                    fr.at[g],
                    head=to_head,
                    batch=to_core,
                ).start()
            rows_all[me_hb, members(g)] = stage[members(g), half(core)]

    ahead = 2
    spread(queries, qs, qr)
    for n in range(ahead):
        pass_on(queries, (qs, qr), fqs, fqr, n, at_turn)

    @pl.loop(0, NZ)
    def _(n):
        @pl.when(n + ahead < NZ)
        def _():
            pass_on(queries, (qs, qr), fqs, fqr, n + ahead, at_turn)

        passed(queries, fqs, fqr, n, at_turn).wait_recv()
        attend(n)

        @pl.when(n >= 2)
        def _():
            merge_x(n - 2)

    merge_x(NZ - 2)
    merge_x(NZ - 1)
    all_of(merged_z.at[pl.ds(0, NZ - 1)], zas, zar).wait_recv()
    average, _ = merged([merged_z[i] for i in range(NZ)])
    attended[x, z] = average.T.astype(bf16)
    spread(attended, ms, mr)
    for n in range(NZ):
        pass_on(attended, (ms, mr), fms, fmr, n, at_step)
    for which in range(parts_of_z):
        project(which)
    dispatch()
    load_gate.wait()
    load_up.wait()
    load_down.wait()
    all_of(queries.at[0, pl.ds(0, NZ - 1)], qs, qr.at[0]).wait_send()
    all_of(queries.at[pl.ds(0, NX - 1)], fqs, fqr.at[0]).wait_send()
    all_of(average_s.at[:, pl.ds(0, NX - 1)], xas, xar.at[0]).wait_send()
    all_of(arrived.at[pl.ds(0, NZ - 1)], ps, pr).wait_send()
    all_of(merged_s.at[pl.ds(0, NZ - 1)], zas, zar).wait_send()
    all_of(attended.at[0, pl.ds(0, NZ - 1)], ms, mr.at[0]).wait_send()
    all_of(attended.at[pl.ds(0, NX - 1)], fms, fmr.at[0]).wait_send()
    all_of(part.at[:, pl.ds(0, NH - 1)], hs, hr.at[0]).wait_send()
    forward()
    all_of(outgoing.at[pl.ds(0, NE - 1)], es, er.at[0]).wait_send()

    held = NH * NB * slots
    square = jnp.zeros((held, features), f32)
    for g in range(groups):
        for e in range(g * per_group, (g + 1) * per_group):
            if e == g * per_group:
                all_of(rows_all.at[pl.ds(0, most), members(g)], fs, fr.at[g]).wait_recv()
            wide = rows_all[:, e].reshape(held, features).astype(f32)
            square = square + wide * wide
    mean = jnp.sum(square, axis=1, keepdims=True) * (1.0 / (NE * features))
    scale = lax.rsqrt(mean + EPSILON)
    for e in range(NE):
        wide = rows_all[:, e].reshape(held, features).astype(f32)
        normed[:, e * features : (e + 1) * features] = (
            wide * scale * post_gain[e : e + 1, :].astype(f32)
        ).astype(bf16)
    gate_part = jnp.dot(normed[...], gate_v[...], preferred_element_type=f32)
    up_part = jnp.dot(normed[...], up_v[...], preferred_element_type=f32)
    hidden = (gate_part / (1.0 + jnp.exp(-gate_part)) * up_part).astype(bf16)
    reach = parts.shape[-1]
    bands = parts.shape[0]
    per_band = NE // bands

    own_band = expert // per_band
    band_order = [lax.rem(own_band + i, bands) for i in (2, 1, 3, 0)]
    for g in band_order:
        lanes = pl.ds(pl.multiple_of(g * reach, reach), reach)
        made = jnp.dot(hidden, down_v[:, lanes], preferred_element_type=f32)
        product[g] = made.astype(bf16).reshape(NH * NB, slots, reach)
        for i, j in others:
            to_head, to_core = target_of(i, j)
            remote(
                product.at[g, to_head * NB + to_core],
                parts.at[g, me_hb],
                gs,
                gr.at[g],
                head=to_head,
                batch=to_core,
            ).start()
        parts[g, me_hb] = product[g, me_hb]

    for g in band_order:
        all_of(parts.at[g, pl.ds(0, most)], gs, gr.at[g]).wait_recv()
        total = parts[g, pl.ds(0, NB)].astype(f32)
        for i in range(1, NH):
            total = total + parts[g, pl.ds(i * NB, NB)].astype(f32)
        total = total.reshape(NB * slots, reach).astype(bf16)
        for k in range(per_band):
            back[g * per_band + k] = total[:, k * features : (k + 1) * features]

        @pl.loop(0, per_band)
        def _(k):
            target = g * per_band + k

            @pl.when(target != expert)
            def _():
                remote(back.at[target], returned.at[expert], bs, br, expert=target).start()

    returned[expert] = back[expert]
    all_of(rows_all.at[pl.ds(0, most)], fs, fr.at[0]).wait_send()
    all_of(product.at[:, pl.ds(0, most)], gs, gr.at[0]).wait_send()
    all_of(returned.at[pl.ds(0, NE - 1)], bs, br).wait_recv()
    both = jnp.dot(
        mixing[...],
        returned[...].reshape(experts * slots, features),
        preferred_element_type=f32,
    )
    mixture = both[:count] + both[count:]
    final_s[...] = (held_stream[...].astype(f32) + mixture).astype(bf16)
    for k in (1, 3, 2):
        remote(final_s, final_r.at[head], ys, yr, head=lax.rem(head + k, NH)).start()
    final_r[head] = final_s[...]
    all_of(back.at[pl.ds(0, NE - 1)], bs, br).wait_send()
    all_of(final_r.at[pl.ds(0, NH - 1)], ys, yr).wait_recv()
    pieces = [final_r[i].astype(f32).reshape(NZ, sub, features) for i in range(NH)]
    out[...] = jnp.concatenate(
        [pieces[i][r] for r in range(NZ) for i in range(NH)], axis=0
    ).astype(bf16)
    all_of(final_r.at[pl.ds(0, NH - 1)], ys, yr).wait_send()


def on_device(
    tokens, attn_gain, w_query, q_gain, cached_keys, prefix_values, output_weight,
    post_gain, routes, route_gates, w_gate, w_up, w_down,
):
    rows, features = tokens.shape
    width = w_query.shape[1] // NX
    block = rows * w_query.shape[1] // HEAD // NE
    bf16, f32 = jnp.bfloat16, jnp.float32
    keys = cached_keys.shape[0]
    span = rows // NZ
    sub = span // NH
    count = NZ * sub
    halves = 2

    model, ff = w_gate.shape[1:]
    slots = 2 * count // 8
    groups = 2
    bands = 4
    experts = NE * NB
    V = pltpu.VMEM
    return pl.pallas_call(
        layer_kernel,
        out_shape=jax.ShapeDtypeStruct((rows, features), bf16),
        in_specs=[IN_VMEM, IN_VMEM, IN_ANY, IN_VMEM] + [IN_ANY] * 3 + [IN_VMEM] * 3 + [IN_ANY] * 3,
        out_specs=IN_VMEM,
        scratch_shapes=[
            V((NX, rows, features), bf16),
            V((NX, features, width), bf16),
            V((NZ, span, width), f32),
            V((NZ, span, width), f32),
            V((NX, NZ, block, HEAD), bf16),
            V((keys, HEAD), bf16),
            V((keys, HEAD), bf16),
            V((HEAD, keys), bf16),
            V(output_weight.shape, bf16),
            V((keys, NX * block), f32),
            V((NZ, NX, HEAD + LOG_ROWS, block), bf16),
            V((NZ, NX, HEAD + LOG_ROWS, block), bf16),
            V((NZ, HEAD + LOG_ROWS, block), bf16),
            V((NZ, HEAD + LOG_ROWS, block), bf16),
            V((NX, NZ, block, HEAD), bf16),
            V((halves, NH, count // halves, features), f32),
            V((halves, NH, count // halves, features), f32),
            V((NZ, sub, features), f32),
            V((count, features), bf16),
            V((experts * slots, count), bf16),
            V((2 * count, experts * slots), bf16),
            V((model, ff), bf16),
            V((model, ff), bf16),
            V((ff, model), bf16),
            V((NE, NB * slots, features), bf16),
            V((NE, NB * slots, features), bf16),
            V((NH * NB, NE, slots, features), bf16),
            V((NH * NB * slots, model), bf16),
            V((bands, NH * NB, slots, model // bands), bf16),
            V((bands, NH * NB, slots, model // bands), bf16),
            V((NE, NB * slots, features), bf16),
            V((NE, NB * slots, features), bf16),
            V((count, features), bf16),
            V((NH, count, features), bf16),
            DMA((7,)),
            DMA, DMA, DMA, DMA, DMA, DMA,
            DMA, DMA,
            DMA, DMA((NZ,)), DMA, DMA((NZ,)),
            DMA, DMA((NZ,)), DMA, DMA,
            DMA, DMA((NZ,)), DMA, DMA((NZ,)),
            DMA, DMA((halves,)),
            DMA, DMA((groups,)), DMA, DMA((groups,)),
            DMA, DMA((bands,)), DMA, DMA, DMA, DMA,
        ],
        compiler_params=pltpu.CompilerParams(
            collective_id=1, has_side_effects=True, vmem_limit_bytes=56 * MIB
        ),
        name="scoring_layer",
    )(
        tokens, attn_gain[None, :], w_query, q_gain[None, :],
        cached_keys, prefix_values, output_weight,
        post_gain.reshape(NE, features), routes.T, route_gates.T,
        w_gate[0], w_up[0], w_down[0],
    )


def solution(mesh):
    placed = (
        P("batch", "expert"),
        P("expert"),
        P("expert", "head"),
        P(),
        P("expert", "head"),
        P("expert", "head"),
        P("head", "expert"),
        P(),
        P("batch", None),
        P("batch", None),
        P(("expert", "batch"), None, "head"),
        P(("expert", "batch"), None, "head"),
        P(("expert", "batch"), "head", None),
    )
    return jax.shard_map(
        on_device, mesh=mesh, in_specs=placed, out_specs=P("batch", "expert"), check_vma=False
    )
```
